1024 devices in a mesh: wide: 64 (over z, core), pan: 4 (over x), rep: 4 (over y).
Axes of the slice: x: 4, y: 4, z: 32, core: 2. Of those that a mesh axis runs over, the one named last changes fastest.
Arguments:
- amplitudes: float32 [8, 1536, 1536], P(None, 'wide', ('pan', 'rep')), may hold values from -0.15625 to 0.15625
- integrals: float32 [8, 1536, 1536], P(None, ('pan', 'rep'), 'wide'), may hold values from -6 to 6
- pair_energies: float32 [8, 1536], replicated, may hold values from 0.5 to 4
- block_sizes: int32 [8], replicated, may hold values from 768 to 1536, as said below
Outputs:
- residual: float32 [8, 1536, 1536], P(None, 'wide')
- update: float32 [8, 1536, 1536], P(None, 'wide')
The draws below stay inside these ranges and needn't reach their ends.
Inputs may be any that keep to these rules, and one draw needn't show every extreme that they name: Block h holds block_sizes[h] live ov pairs, the leading slots of its 1536; some block holds exactly 1536.
All inputs are finite; a program needn't handle non-finite values.
Results may differ from the reference program's by a relative error of at most 0.000071.
Values sent between devices are 32-bit elements; how exact they have to be, the bound alone decides.
A program may use at most 64 MiB of HBM per device.

```python
import math
import jax
import jax.numpy as jnp
from jax import lax

NSYM = 8
CAP = 1536


def draw_block_sizes(key, part):
    key = jax.random.fold_in(key, 7)
    first, second = jax.random.split(key)
    sizes = jax.random.randint(first, (NSYM,), CAP // 2, CAP + 1, dtype=jnp.int32)
    largest = jax.random.randint(second, (), 0, NSYM, dtype=jnp.int32)
    return jnp.where(jnp.arange(NSYM, dtype=jnp.int32) == largest, CAP, sizes).astype(jnp.int32)


def level_of(key, dims, shards, least, high):
    def one(dim, parts):
        draws = jax.random.uniform(jax.random.fold_in(jax.random.fold_in(key, 6), dim), (parts,), jnp.float32, least / len(shards), high / len(shards))
        return jnp.repeat(jnp.exp(draws), dims[dim] // parts).reshape((-1,) + (1,) * (len(dims) - dim - 1))

    loudness = one(*shards[0])
    for cut in shards[1:]:
        loudness = loudness * one(*cut)
    return loudness


def noise(own_key, dims, spread, most, cuts=(), kind=jnp.bfloat16):
    drawn = spread * jax.random.normal(own_key, dims, jnp.float32)
    if cuts:
        drawn = drawn * level_of(own_key, dims, cuts, -0.22, 0.18)
    return jnp.clip(drawn, -most, most).astype(kind)


def setup_inputs(seed: int = 0) -> dict:
    keys = jax.random.split(jax.random.key(seed), 5)
    return {
        "amplitudes": noise(keys[0], (NSYM, CAP, CAP), CAP ** -0.5, 0.15625, ((1, 64), (2, 16)), jnp.float32),
        "integrals": noise(keys[1], (NSYM, CAP, CAP), 1.0, 6.0, ((1, 16), (2, 64)), jnp.float32),
        "pair_energies": jnp.clip(jnp.exp(jax.random.uniform(keys[2], (NSYM, CAP), jnp.float32, math.log(0.5), math.log(4.0))), 0.5, 4.0),
        "block_sizes": draw_block_sizes(jax.random.fold_in(keys[4], 71), 0),
    }


def reference(amplitudes, integrals, pair_energies, block_sizes):
    position = jnp.arange(CAP, dtype=jnp.int32)
    live_mask = (position[None, :] < block_sizes[:, None]).astype(jnp.float32)
    amp_live = amplitudes * live_mask[:, :, None] * live_mask[:, None, :]
    int_live = integrals * live_mask[:, :, None] * live_mask[:, None, :]
    cycle = jnp.einsum("hpk,hkq->hpq", amp_live, int_live, precision=lax.Precision.HIGHEST)
    residual = cycle + jnp.swapaxes(cycle, 1, 2)
    denominator = pair_energies[:, :, None] + pair_energies[:, None, :]
    update = -residual / denominator
    return residual, update
```

```python
import jax
import jax.numpy as jnp
from jax import lax
from jax.experimental import pallas as pl
from jax.experimental.pallas import tpu as pltpu
from jax.sharding import PartitionSpec as P

MESH = pl.DeviceIdType.MESH


def cycle_kernel(
    sizes_ref, amp_ref, int_ref, out_ref,
    stage, held, amp_all, int_all, part, parts, block_out, block_in, rows_out,
    send1, recv1, send_a, recv_a, send_b, recv_b, send_c, recv_c,
    send3, recv3, send4, recv4, send5, recv5, send6, recv6, send7, recv7,
):
    wide, pan, rep = lax.axis_index("wide"), lax.axis_index("pan"), lax.axis_index("rep")
    z, core = wide // 2, wide % 2
    owner, layer = z // 4, z % 4
    band, rank = z // 8, z % 8

    def device(w, x, y):
        return {"wide": w, "pan": x, "rep": y}

    def remote(src, dst, ssem, rsem, to):
        return pltpu.make_async_remote_copy(
            src_ref=src, dst_ref=dst, send_sem=ssem, recv_sem=rsem,
            device_id=device(*to), device_id_type=MESH,
        )

    def is_me(to):
        return (to[0] == wide) & (to[1] == pan) & (to[2] == rep)

    def start(src, dst, ssem, rsem, to):
        me = is_me(to)

        @pl.when(me)
        def _():
            pltpu.make_async_copy(src, dst, rsem).start()

        @pl.when(jnp.logical_not(me))
        def _():
            remote(src, dst, ssem, rsem, to).start()

    def finish_send(src, dst, ssem, rsem, to):
        @pl.when(jnp.logical_not(is_me(to)))
        def _():
            remote(src, dst, ssem, rsem, to).wait_send()

    def arrived(dst, rsem):
        pltpu.make_async_copy(dst, dst, rsem).wait()

    row_at = wide * 24 + lax.broadcasted_iota(jnp.int32, (24, 96), 0)
    sum_at = (pan * 4 + rep) * 96 + lax.broadcasted_iota(jnp.int32, (24, 96), 1)
    stage[...] = jnp.zeros_like(stage)
    for h in range(8):
        live = (row_at < sizes_ref[h]) & (sum_at < sizes_ref[h])
        stage[h, 0:24, 0:96] = jnp.where(live, amp_ref[h], 0.0)
        stage[h, 24:48, 0:96] = jnp.where(live, int_ref[h], 0.0)

    slot1 = (rank % 4) * 2 + core
    sends1 = []
    for step in range(8):
        h = (owner + step) % 8
        to = (2 * (4 * h + band) + rank // 4, pan, rep)
        sends1.append((stage.at[h], held.at[slot1], send1.at[step], recv1.at[slot1], to))
        start(*sends1[-1])
    for i in range(8):
        arrived(held.at[i], recv1.at[i])

    sends2 = []
    for step in range(1, 4):
        y = (rep + step) % 4
        sends2.append((held.at[:, 0:24], amp_all.at[rep], send_a.at[step], recv_a.at[rep], (wide, pan, y)))
        remote(*sends2[-1]).start()
    sends2b = []
    for step in range(4):
        to = (2 * (4 * owner + (layer + step) % 4) + core, pan, layer)
        sends2b.append((held.at[:, 24:48], int_all.at[core, rep], send_b.at[step], recv_b.at[rep], to))
        start(*sends2b[-1])
    own_amp = pltpu.make_async_copy(held.at[:, 0:24], amp_all.at[rep], send_a.at[0])
    own_amp.start()
    sends2c = []
    for y in range(4):
        arrived(int_all.at[core, y], recv_b.at[y])
        sends2c.append((int_all.at[core, y], int_all.at[core, y], send_c.at[y], recv_c.at[y], (2 * z + 1 - core, pan, rep)))
        remote(*sends2c[-1]).start()
    own_amp.wait()
    for step in range(1, 4):
        y = (rep + step) % 4
        arrived(amp_all.at[y], recv_a.at[y])
    for y in range(4):
        arrived(int_all.at[1 - core, y], recv_c.at[y])

    for side in range(2):
        total = jnp.zeros((192, 192), jnp.float32)
        for y in range(4):
            total = total + lax.dot_general(
                amp_all[y].reshape(192, 128), int_all[side, y].reshape(192, 128),
                (((1,), (1,)), ((), ())), precision=lax.Precision.HIGHEST, preferred_element_type=jnp.float32,
            )
        part[:, 192 * side:192 * (side + 1)] = total
    sends3 = []
    for step in range(1, 4):
        x = (pan + step) % 4
        rows = part.at[pl.ds(pl.multiple_of(48 * x, 8), 48)]
        sends3.append((rows, parts.at[pan], send3.at[step], recv3.at[pan], (wide, x, rep)))
        remote(*sends3[-1]).start()
    parts[pan] = part[pl.ds(pl.multiple_of(48 * pan, 8), 48)]
    for step in range(1, 4):
        x = (pan + step) % 4
        arrived(parts.at[x], recv3.at[x])
    cycle = parts[0] + parts[1] + parts[2] + parts[3]

    flipped = jnp.concatenate([cycle, jnp.zeros((80, 384), jnp.float32)], axis=0).T
    block_out[...] = flipped.reshape(8, 48, 128)
    mine = 4 * core + pan
    sends4 = []
    for step in range(8):
        b = (mine + step) % 8
        to = (2 * (4 * owner + rep) + b // 4, b % 4, layer)
        sends4.append((block_out.at[b], block_in.at[mine], send4.at[step], recv4.at[mine], to))
        start(*sends4[-1])
    mirror = jnp.zeros((48, 384), jnp.float32)
    for b in range(8):
        arrived(block_in.at[b], recv4.at[b])
        widened = jnp.concatenate([block_in[b], jnp.zeros((48, 256), jnp.float32)], axis=1)
        mirror = mirror + (pltpu.roll(widened, 48 * b, 1) if b else widened)
    rows_out[...] = cycle + mirror

    columns = pl.ds(pl.multiple_of(384 * rep, 128), 384)
    sends5 = []
    for c in range(2):
        to = (2 * (8 * layer + 4 * core + pan) + c, (owner + layer) % 4, rep)
        sends5.append((rows_out.at[24 * c:24 * (c + 1)], out_ref.at[owner, :, columns], send5.at[c], recv5.at[owner // 4], to))
        start(*sends5[-1])

    first = (pan + 4 - band) % 4
    sends6 = []
    arrived(out_ref.at[first, :, columns], recv5.at[0])
    for step in range(1, 4):
        to = (wide, pan, (rep + step) % 4)
        here = out_ref.at[first, :, columns]
        sends6.append((here, here, send6.at[0, step], recv6.at[0, rep], to))
        remote(*sends6[-1]).start()
    arrived(out_ref.at[first + 4, :, columns], recv5.at[1])
    for step in range(1, 4):
        to = (wide, (pan + step) % 4, rep)
        here = out_ref.at[first + 4, :, columns]
        sends6.append((here, here, send6.at[1, step], recv6.at[1, pan], to))
        remote(*sends6[-1]).start()
    for step in range(1, 4):
        y = (rep + step) % 4
        arrived(out_ref.at[first, :, pl.ds(pl.multiple_of(384 * y, 128), 384)], recv6.at[0, y])
    sends7 = []
    for step in range(1, 4):
        to = (wide, (pan + step) % 4, rep)
        here = out_ref.at[first]
        sends7.append((here, here, send7.at[0, step], recv7.at[0, pan], to))
        remote(*sends7[-1]).start()
    for step in range(1, 4):
        x = (pan + step) % 4
        arrived(out_ref.at[(x + 4 - band) % 4 + 4, :, columns], recv6.at[1, x])
    for step in range(1, 4):
        to = (wide, pan, (rep + step) % 4)
        here = out_ref.at[4:8, :, columns]
        sends7.append((here, here, send7.at[1, step], recv7.at[1, rep], to))
        remote(*sends7[-1]).start()
    for step in range(1, 4):
        x = (pan + step) % 4
        arrived(out_ref.at[(x + 4 - band) % 4], recv7.at[0, x])
    for step in range(1, 4):
        y = (rep + step) % 4
        arrived(out_ref.at[4:8, :, pl.ds(pl.multiple_of(384 * y, 128), 384)], recv7.at[1, y])

    for args in sends1 + sends2b + sends4 + sends5:
        finish_send(*args)
    for args in sends2 + sends2c + sends3 + sends6 + sends7:
        remote(*args).wait_send()


def shards(amplitudes, integrals, pair_energies, block_sizes):
    vmem = pl.BlockSpec(memory_space=pltpu.VMEM)
    dma = pltpu.SemaphoreType.DMA
    residual = pl.pallas_call(
        cycle_kernel,
        out_shape=jax.ShapeDtypeStruct((8, 24, 1536), jnp.float32),
        in_specs=[pl.BlockSpec(memory_space=pltpu.SMEM), vmem, vmem],
        out_specs=vmem,
        scratch_shapes=[
            pltpu.VMEM((8, 48, 128), jnp.float32),
            pltpu.VMEM((8, 48, 128), jnp.float32),
            pltpu.VMEM((4, 8, 24, 128), jnp.float32),
            pltpu.VMEM((2, 4, 8, 24, 128), jnp.float32),
            pltpu.VMEM((192, 384), jnp.float32),
            pltpu.VMEM((4, 48, 384), jnp.float32),
            pltpu.VMEM((8, 48, 128), jnp.float32),
            pltpu.VMEM((8, 48, 128), jnp.float32),
            pltpu.VMEM((48, 384), jnp.float32),
            dma((8,)), dma((8,)),
            dma((4,)), dma((4,)), dma((4,)), dma((4,)), dma((4,)), dma((4,)),
            dma((4,)), dma((4,)), dma((8,)), dma((8,)), dma((2,)), dma((2,)),
            dma((2, 4)), dma((2, 4)), dma((2, 4)), dma((2, 4)),
        ],
        compiler_params=pltpu.CompilerParams(has_side_effects=True, vmem_limit_bytes=24 * 1024 * 1024),
        cost_estimate=pl.CostEstimate(flops=60_000_000, bytes_accessed=2_000_000, transcendentals=0),
    )(block_sizes, amplitudes, jnp.swapaxes(integrals, 1, 2))
    row_start = lax.axis_index("wide") * 24
    energy_rows = lax.dynamic_slice_in_dim(pair_energies, row_start, 24, 1)
    update = -residual / (energy_rows[:, :, None] + pair_energies[:, None, :])
    return (residual, update)


def solution(mesh):
    in_specs = (P(None, "wide", ("pan", "rep")), P(None, ("pan", "rep"), "wide"), P(), P())
    out_specs = (P(None, "wide", None), P(None, "wide", None))
    return jax.shard_map(shards, mesh=mesh, in_specs=in_specs, out_specs=out_specs, check_vma=False)
```

```python
import jax
import jax.numpy as jnp
from jax import lax
from jax.experimental import pallas as pl
from jax.experimental.pallas import tpu as pltpu
from jax.sharding import PartitionSpec as P

MESH = pl.DeviceIdType.MESH


def cycle_kernel(
    sizes_ref, amp_hbm, int_hbm, out_ref,
    amp_ref, int_ref, stage, held_packed, held, amp_all, int_all, part, parts, block_out, block_in, rows_out,
    load, send1, recv1, send_a, recv_a, send_b, recv_b, send_c, recv_c,
    send3, recv3, send4, recv4, send5, recv5, send6, recv6, send7, recv7,
):
    wide, pan, rep = lax.axis_index("wide"), lax.axis_index("pan"), lax.axis_index("rep")
    z, core = wide // 2, wide % 2
    owner, layer = z // 4, z % 4
    band, rank = z // 8, z % 8

    def device(w, x, y):
        return {"wide": w, "pan": x, "rep": y}

    def remote(src, dst, ssem, rsem, to):
        return pltpu.make_async_remote_copy(
            src_ref=src, dst_ref=dst, send_sem=ssem, recv_sem=rsem,
            device_id=device(*to), device_id_type=MESH,
        )

    def is_me(to):
        return (to[0] == wide) & (to[1] == pan) & (to[2] == rep)

    def start(src, dst, ssem, rsem, to):
        me = is_me(to)

        @pl.when(me)
        def _():
            pltpu.make_async_copy(src, dst, rsem).start()

        @pl.when(jnp.logical_not(me))
        def _():
            remote(src, dst, ssem, rsem, to).start()

    def finish_send(src, dst, ssem, rsem, to):
        @pl.when(jnp.logical_not(is_me(to)))
        def _():
            remote(src, dst, ssem, rsem, to).wait_send()

    def arrived(dst, rsem):
        pltpu.make_async_copy(dst, dst, rsem).wait()

    sends1, sends2, sends2b, sends2c, sends3, sends4, sends5, sends6, sends7 = [[] for _ in range(9)]

    def drain():
        for args in sends1 + sends2b + sends4 + sends5:
            finish_send(*args)
        for args in sends2 + sends2c + sends3 + sends6 + sends7:
            remote(*args).wait_send()

    loads = [
        pltpu.make_async_copy(amp_hbm, amp_ref, load.at[0]),
        pltpu.make_async_copy(int_hbm, int_ref, load.at[1]),
    ]
    for copy in loads:
        copy.start()

    first = (pan + 4 - z % 4) % 4
    callers = [(2 * (8 * layer + 4 * core + i // 2) + i % 2, pan, rep) for i in range(8)]
    callers += [(wide, pan, (rep + step) % 4) for step in range(1, 4)]
    callers += [(wide, (pan + step) % 4, rep) for step in range(1, 4)]
    callers += [(2 * z + 1 - core, pan, rep)]
    callers += [(2 * (4 * owner + rep) + core, pan, y) for y in range(4)]
    callers += [(2 * (4 * owner + rep) + b // 4, b % 4, layer) for b in range(8)]
    callers += [(2 * (4 * (first + 4 * i) + band) + rank // 4, z % 4, rep) for i in range(2)]
    barrier = pltpu.get_barrier_semaphore()
    for to in callers:
        pl.semaphore_signal(barrier, inc=1, device_id=device(*to), device_id_type=MESH)

    row_at = wide * 24 + lax.broadcasted_iota(jnp.int32, (24, 128), 0)
    lane = lax.broadcasted_iota(jnp.int32, (24, 128), 1)
    sum_at = (pan * 4 + rep) * 96 + lane
    lane8 = lane[0:8]
    for copy in loads:
        copy.wait()
    for h in range(8):
        live = (row_at < sizes_ref[h]) & (sum_at < sizes_ref[h]) & (lane < 96)
        tails = []
        for side, ref in enumerate((amp_ref, int_ref)):
            value = jnp.concatenate([ref[h], jnp.zeros((24, 32), jnp.float32)], axis=1)
            value = jnp.where(live, value, 0.0)
            last = value[16:24]
            stage[h, 16 * side:16 * side + 8] = jnp.where(lane8 < 96, value[0:8], pltpu.roll(last, 96, 1))
            stage[h, 16 * side + 8:16 * side + 16] = jnp.where(lane8 < 96, value[8:16], pltpu.roll(last, 64, 1))
            tail = pltpu.roll(last, 64, 1)
            tails.append(jnp.where(lane8 < 32, tail, pltpu.roll(pltpu.roll(tail, 32, 1), 4, 0)))
        stage[h, 32:36] = jnp.where(lane8 < 64, tails[0], pltpu.roll(tails[1], 64, 1))[0:4]
    pl.semaphore_wait(barrier, len(callers))

    slot1 = (rank % 4) * 2 + core
    for step in range(8):
        h = (owner + step) % 8
        to = (2 * (4 * h + band) + rank // 4, pan, rep)
        sends1.append((stage.at[h], held_packed.at[slot1], send1.at[step], recv1.at[slot1], to))
        start(*sends1[-1])
    for i in range(8):
        arrived(held_packed.at[i], recv1.at[i])
        four = jnp.concatenate([held_packed[i, 32:36], jnp.zeros((4, 128), jnp.float32)], axis=0)
        for side in range(2):
            one, two = held_packed[i, 16 * side:16 * side + 8], held_packed[i, 16 * side + 8:16 * side + 16]
            tail = pltpu.roll(four, 64, 1) if side else four
            row8 = lax.broadcasted_iota(jnp.int32, (8, 128), 0)
            low = pltpu.roll(tail, 64, 1)
            high = pltpu.roll(pltpu.roll(tail, 32, 1), 4, 0)
            last = jnp.where(row8 < 4, low, high)
            last = jnp.where(lane8 < 64, pltpu.roll(two, 64, 1), last)
            last = jnp.where(lane8 < 32, pltpu.roll(one, 32, 1), last)
            for start_row, value in ((0, one), (8, two), (16, last)):
                held[i, 24 * side + start_row:24 * side + start_row + 8] = jnp.where(lane8 < 96, value, 0.0)

    for step in range(1, 4):
        y = (rep + step) % 4
        sends2.append((held.at[:, 0:24], amp_all.at[rep], send_a.at[step], recv_a.at[rep], (wide, pan, y)))
        remote(*sends2[-1]).start()
    for step in range(4):
        to = (2 * (4 * owner + (layer + step) % 4) + core, pan, layer)
        sends2b.append((held.at[:, 24:48], int_all.at[core, rep], send_b.at[step], recv_b.at[rep], to))
        start(*sends2b[-1])
    own_amp = pltpu.make_async_copy(held.at[:, 0:24], amp_all.at[rep], send_a.at[0])
    own_amp.start()
    for y in range(4):
        arrived(int_all.at[core, y], recv_b.at[y])
        sends2c.append((int_all.at[core, y], int_all.at[core, y], send_c.at[y], recv_c.at[y], (2 * z + 1 - core, pan, rep)))
        remote(*sends2c[-1]).start()
    own_amp.wait()
    for step in range(1, 4):
        y = (rep + step) % 4
        arrived(amp_all.at[y], recv_a.at[y])
    for y in range(4):
        arrived(int_all.at[1 - core, y], recv_c.at[y])

    for side in range(2):
        total = jnp.zeros((192, 192), jnp.float32)
        for y in range(4):
            total = total + lax.dot_general(
                amp_all[y].reshape(192, 128), int_all[side, y].reshape(192, 128),
                (((1,), (1,)), ((), ())), precision=lax.Precision.HIGHEST, preferred_element_type=jnp.float32,
            )
        part[:, 192 * side:192 * (side + 1)] = total
    for step in range(1, 4):
        x = (pan + step) % 4
        rows = part.at[pl.ds(pl.multiple_of(48 * x, 8), 48)]
        sends3.append((rows, parts.at[pan], send3.at[step], recv3.at[pan], (wide, x, rep)))
        remote(*sends3[-1]).start()
    parts[pan] = part[pl.ds(pl.multiple_of(48 * pan, 8), 48)]
    for step in range(1, 4):
        x = (pan + step) % 4
        arrived(parts.at[x], recv3.at[x])
    cycle = parts[0] + parts[1] + parts[2] + parts[3]

    flipped = jnp.concatenate([cycle, jnp.zeros((80, 384), jnp.float32)], axis=0).T.reshape(8, 2, 24, 128)
    right = pltpu.roll(flipped[:, 1].reshape(192, 128), 48, 1)
    block_out[...] = flipped[:, 0] + right.reshape(8, 24, 128)
    mine = 4 * core + pan
    for step in range(8):
        b = (mine + step) % 8
        to = (2 * (4 * owner + rep) + b // 4, b % 4, layer)
        sends4.append((block_out.at[b], block_in.at[mine], send4.at[step], recv4.at[mine], to))
        start(*sends4[-1])
    top, bottom = jnp.zeros((24, 384), jnp.float32), jnp.zeros((24, 384), jnp.float32)
    wide_lane = lax.broadcasted_iota(jnp.int32, (24, 384), 1)
    for b in range(8):
        arrived(block_in.at[b], recv4.at[b])
        both = jnp.concatenate([block_in[b], jnp.zeros((24, 256), jnp.float32)], axis=1)
        above = jnp.where(wide_lane < 48, both, 0.0)
        top = top + (pltpu.roll(above, 48 * b, 1) if b else above)
        below = both - above
        bottom = bottom + (pltpu.roll(below, (48 * b + 336) % 384, 1) if b != 1 else below)
    rows_out[0:24] = cycle[0:24] + top
    rows_out[24:48] = cycle[24:48] + bottom

    columns = pl.ds(pl.multiple_of(384 * rep, 128), 384)
    for c in range(2):
        to = (2 * (8 * layer + 4 * core + pan) + c, (owner + pan) % 4, rep)
        sends5.append((rows_out.at[24 * c:24 * (c + 1)], out_ref.at[owner, :, columns], send5.at[c], recv5.at[owner // 4], to))
        start(*sends5[-1])

    arrived(out_ref.at[first, :, columns], recv5.at[0])
    for step in range(1, 4):
        to = (wide, pan, (rep + step) % 4)
        here = out_ref.at[first, :, columns]
        sends6.append((here, here, send6.at[0, step], recv6.at[0, rep], to))
        remote(*sends6[-1]).start()
    arrived(out_ref.at[first + 4, :, columns], recv5.at[1])
    for step in range(1, 4):
        to = (wide, (pan + step) % 4, rep)
        here = out_ref.at[first + 4, :, columns]
        sends6.append((here, here, send6.at[1, step], recv6.at[1, pan], to))
        remote(*sends6[-1]).start()
    for step in range(1, 4):
        y = (rep + step) % 4
        arrived(out_ref.at[first, :, pl.ds(pl.multiple_of(384 * y, 128), 384)], recv6.at[0, y])
    for step in range(1, 4):
        to = (wide, (pan + step) % 4, rep)
        here = out_ref.at[first]
        sends7.append((here, here, send7.at[0, step], recv7.at[0, pan], to))
        remote(*sends7[-1]).start()
    for step in range(1, 4):
        x = (pan + step) % 4
        arrived(out_ref.at[(x + 4 - z % 4) % 4 + 4, :, columns], recv6.at[1, x])
    for step in range(1, 4):
        to = (wide, pan, (rep + step) % 4)
        here = out_ref.at[4:8, :, columns]
        sends7.append((here, here, send7.at[1, step], recv7.at[1, rep], to))
        remote(*sends7[-1]).start()
    for step in range(1, 4):
        x = (pan + step) % 4
        arrived(out_ref.at[(x + 4 - z % 4) % 4], recv7.at[0, x])
    for step in range(1, 4):
        y = (rep + step) % 4
        arrived(out_ref.at[4:8, :, pl.ds(pl.multiple_of(384 * y, 128), 384)], recv7.at[1, y])

    drain()


def shards(amplitudes, integrals, pair_energies, block_sizes):
    vmem = pl.BlockSpec(memory_space=pltpu.VMEM)
    hbm = pl.BlockSpec(memory_space=pl.ANY)
    dma = pltpu.SemaphoreType.DMA
    residual = pl.pallas_call(
        cycle_kernel,
        out_shape=jax.ShapeDtypeStruct((8, 24, 1536), jnp.float32),
        in_specs=[pl.BlockSpec(memory_space=pltpu.SMEM), hbm, hbm],
        out_specs=vmem,
        scratch_shapes=[
            pltpu.VMEM((8, 24, 96), jnp.float32),
            pltpu.VMEM((8, 24, 96), jnp.float32),
            pltpu.VMEM((8, 36, 128), jnp.float32),
            pltpu.VMEM((8, 36, 128), jnp.float32),
            pltpu.VMEM((8, 48, 128), jnp.float32),
            pltpu.VMEM((4, 8, 24, 128), jnp.float32),
            pltpu.VMEM((2, 4, 8, 24, 128), jnp.float32),
            pltpu.VMEM((192, 384), jnp.float32),
            pltpu.VMEM((4, 48, 384), jnp.float32),
            pltpu.VMEM((8, 24, 128), jnp.float32),
            pltpu.VMEM((8, 24, 128), jnp.float32),
            pltpu.VMEM((48, 384), jnp.float32),
            dma((2,)), dma((8,)), dma((8,)),
            dma((4,)), dma((4,)), dma((4,)), dma((4,)), dma((4,)), dma((4,)),
            dma((4,)), dma((4,)), dma((8,)), dma((8,)), dma((2,)), dma((2,)),
            dma((2, 4)), dma((2, 4)), dma((2, 4)), dma((2, 4)),
        ],
        compiler_params=pltpu.CompilerParams(collective_id=0, has_side_effects=True, vmem_limit_bytes=24 * 1024 * 1024),
        cost_estimate=pl.CostEstimate(flops=60_000_000, bytes_accessed=2_000_000, transcendentals=0),
    )(block_sizes, amplitudes, jnp.swapaxes(integrals, 1, 2))
    row_start = lax.axis_index("wide") * 24
    energy_rows = lax.dynamic_slice_in_dim(pair_energies, row_start, 24, 1)
    update = -residual / (energy_rows[:, :, None] + pair_energies[:, None, :])
    return (residual, update)


def solution(mesh):
    in_specs = (P(None, "wide", ("pan", "rep")), P(None, ("pan", "rep"), "wide"), P(), P())
    out_specs = (P(None, "wide", None), P(None, "wide", None))
    return jax.shard_map(shards, mesh=mesh, in_specs=in_specs, out_specs=out_specs, check_vma=False)
```

```python
import jax
import jax.numpy as jnp
from jax import lax
from jax.experimental import pallas as pl
from jax.experimental.pallas import tpu as pltpu
from jax.sharding import PartitionSpec as P

MESH = pl.DeviceIdType.MESH


def cycle_kernel(
    sizes_ref, amp_hbm, int_hbm, out_ref,
    amp_ref, int_ref, stage, amp_packed, int_packed, amp_all, int_all, part, parts, block_out, block_in, rows_out,
    load, send1, recv1, send_a, recv_a, send_b, recv_b, send_c, recv_c,
    send3, recv3, send4, recv4, send5, recv5, send6, recv6, send7, recv7, send8, recv8,
):
    wide, pan, rep = lax.axis_index("wide"), lax.axis_index("pan"), lax.axis_index("rep")
    z, core = wide // 2, wide % 2
    owner, layer = z // 4, z % 4
    band, rank = z // 8, z % 8

    def device(w, x, y):
        return {"wide": w, "pan": x, "rep": y}

    def remote(src, dst, ssem, rsem, to):
        return pltpu.make_async_remote_copy(
            src_ref=src, dst_ref=dst, send_sem=ssem, recv_sem=rsem,
            device_id=device(*to), device_id_type=MESH,
        )

    def is_me(to):
        return (to[0] == wide) & (to[1] == pan) & (to[2] == rep)

    def start(src, dst, ssem, rsem, to):
        me = is_me(to)

        @pl.when(me)
        def _():
            pltpu.make_async_copy(src, dst, rsem).start()

        @pl.when(jnp.logical_not(me))
        def _():
            remote(src, dst, ssem, rsem, to).start()

    def finish_send(src, dst, ssem, rsem, to):
        @pl.when(jnp.logical_not(is_me(to)))
        def _():
            remote(src, dst, ssem, rsem, to).wait_send()

    def arrived(dst, rsem):
        pltpu.make_async_copy(dst, dst, rsem).wait()

    sent, sent_or_kept = [], []

    def send(*args):
        sent.append(args)
        remote(*args).start()

    def send_or_keep(*args):
        sent_or_kept.append(args)
        start(*args)

    loads = [
        pltpu.make_async_copy(amp_hbm, amp_ref, load.at[0]),
        pltpu.make_async_copy(int_hbm, int_ref, load.at[1]),
    ]
    for copy in loads:
        copy.start()

    first = (pan + 4 - z % 4) % 4
    callers = [(2 * (8 * layer + 4 * core + i // 2) + i % 2, pan, rep) for i in range(8)]
    callers += [(2 * (8 * rep + 4 * core + i // 2) + i % 2, pan, layer) for i in range(8)]
    callers += [(wide, pan, (rep + step) % 4) for step in range(1, 4)]
    callers += [(wide, (pan + step) % 4, rep) for step in range(1, 4)]
    callers += [(2 * z + 1 - core, pan, rep)]
    callers += [(2 * (4 * owner + (layer + step) % 4) + core, pan, rep) for step in range(1, 4)]
    callers += [(2 * (4 * owner + rep) + b // 4, b % 4, layer) for b in range(8)]
    callers += [(2 * (4 * (first + 4 * i) + band) + rank // 4, z % 4, rep) for i in range(2)]
    barrier = pltpu.get_barrier_semaphore()
    for to in callers:
        pl.semaphore_signal(barrier, inc=1, device_id=device(*to), device_id_type=MESH)

    row_at = wide * 24 + lax.broadcasted_iota(jnp.int32, (24, 128), 0)
    lane = lax.broadcasted_iota(jnp.int32, (24, 128), 1)
    sum_at = (pan * 4 + rep) * 96 + lane
    lane8 = lane[0:8]
    for copy in loads:
        copy.wait()
    for h in range(8):
        live = (row_at < sizes_ref[h]) & (sum_at < sizes_ref[h]) & (lane < 96)
        for side, ref in enumerate((amp_ref, int_ref)):
            value = jnp.concatenate([ref[h], jnp.zeros((24, 32), jnp.float32)], axis=1)
            value = jnp.where(live, value, 0.0)
            last = value[16:24]
            stage[side, h, 0:8] = jnp.where(lane8 < 96, value[0:8], pltpu.roll(last, 96, 1))
            stage[side, h, 8:16] = jnp.where(lane8 < 96, value[8:16], pltpu.roll(last, 64, 1))
            pairs = pltpu.roll(last, 64, 1)
            pairs = jnp.where(lane8 < 32, pairs, pltpu.roll(pltpu.roll(last, 96, 1), 6, 0))
            pairs = jnp.where(lane8 < 64, pairs, pltpu.roll(last, 4, 0))
            pairs = jnp.where(lane8 < 96, pairs, pltpu.roll(pltpu.roll(last, 32, 1), 2, 0))
            stage[side, h, 16:18] = pairs[0:2]
    pl.semaphore_wait(barrier, len(callers))

    slot1 = (rank % 4) * 2 + core
    for step in (4, 3, 5, 2, 6, 1, 7, 0):
        h = (owner + step) % 8
        to = (2 * (4 * h + band) + rank // 4, pan, rep)
        send_or_keep(stage.at[0, h], amp_packed.at[rep, slot1], send1.at[0, step], recv1.at[0, slot1], to)
        to = (2 * (4 * h + rep) + rank // 4, pan, band)
        send_or_keep(stage.at[1, h], int_packed.at[rank // 4, rep, slot1], send1.at[1, step], recv1.at[1, slot1], to)

    sibling = (2 * z + 1 - core, pan, rep)
    for pair in range(4):
        two = slice(2 * pair, 2 * pair + 2)
        for i in (2 * pair, 2 * pair + 1):
            arrived(amp_packed.at[rep, i], recv1.at[0, i])
        here = amp_packed.at[rep, two]
        for step in range(1, 4):
            send(here, here, send_a.at[pair, step], recv_a.at[pair, rep], (wide, pan, (rep + step) % 4))
        for i in (2 * pair, 2 * pair + 1):
            arrived(int_packed.at[core, layer, i], recv1.at[1, i])
        here = int_packed.at[core, layer, two]
        for step in range(1, 4):
            to = (2 * (4 * owner + (layer + step) % 4) + core, pan, rep)
            send(here, here, send_b.at[pair, step], recv_b.at[pair, layer], to)
        send(here, here, send_c.at[pair, 0], recv_c.at[pair, layer], sibling)

    def unpack(packed, whole, index, mask):
        for i in range(8):
            one, two = packed[index + (i, slice(0, 8))], packed[index + (i, slice(8, 16))]
            tail = jnp.concatenate([packed[index + (i, slice(16, 18))], jnp.zeros((6, 128), jnp.float32)], axis=0)
            last = pltpu.roll(tail, 64, 1) + pltpu.roll(pltpu.roll(tail, 32, 1), 2, 0)
            last = last + pltpu.roll(tail, 4, 0) + pltpu.roll(pltpu.roll(tail, 96, 1), 6, 0)
            last = jnp.where(lane8 < 64, pltpu.roll(two, 64, 1), last)
            last = jnp.where(lane8 < 32, pltpu.roll(one, 32, 1), last)
            for row, value in ((0, one), (8, two), (16, last)):
                whole[index + (slice(24 * i + row, 24 * i + row + 8),)] = jnp.where(lane8 < 96, value, 0.0) if mask else value

    unpack(amp_packed, amp_all, (rep,), True)
    unpack(int_packed, int_all, (core, layer), False)
    for step in (1, 3, 2):
        y, l = (rep + step) % 4, (layer + step) % 4
        for pair in range(4):
            two = slice(2 * pair, 2 * pair + 2)
            arrived(int_packed.at[core, l, two], recv_b.at[pair, l])
            here = int_packed.at[core, l, two]
            send(here, here, send_c.at[pair, step], recv_c.at[pair, l], sibling)
        unpack(int_packed, int_all, (core, l), False)
        for pair in range(4):
            arrived(amp_packed.at[y, 2 * pair:2 * pair + 2], recv_a.at[pair, y])
        unpack(amp_packed, amp_all, (y,), True)
    for step in (0, 1, 3, 2):
        l = (layer + step) % 4
        for pair in range(4):
            arrived(int_packed.at[1 - core, l, 2 * pair:2 * pair + 2], recv_c.at[pair, l])
        unpack(int_packed, int_all, (1 - core, l), False)

    for side in range(2):
        total = jnp.zeros((192, 192), jnp.float32)
        for y in range(4):
            total = total + lax.dot_general(
                amp_all[y], int_all[side, y],
                (((1,), (1,)), ((), ())), precision=lax.Precision.HIGHEST, preferred_element_type=jnp.float32,
            )
        part[:, 192 * side:192 * (side + 1)] = total
    for step in range(1, 4):
        x = (pan + step) % 4
        rows = part.at[pl.ds(pl.multiple_of(48 * x, 8), 48)]
        send(rows, parts.at[pan], send3.at[step], recv3.at[pan], (wide, x, rep))
    parts[pan] = part[pl.ds(pl.multiple_of(48 * pan, 8), 48)]
    for step in range(1, 4):
        x = (pan + step) % 4
        arrived(parts.at[x], recv3.at[x])
    cycle = parts[0] + parts[1] + parts[2] + parts[3]

    flipped = jnp.concatenate([cycle, jnp.zeros((80, 384), jnp.float32)], axis=0).T.reshape(8, 2, 24, 128)
    right = pltpu.roll(flipped[:, 1].reshape(192, 128), 48, 1)
    block_out[...] = flipped[:, 0] + right.reshape(8, 24, 128)
    mine = 4 * core + pan
    for step in range(8):
        b = (mine + step) % 8
        to = (2 * (4 * owner + rep) + b // 4, b % 4, layer)
        send_or_keep(block_out.at[b], block_in.at[mine], send4.at[step], recv4.at[mine], to)
    top, bottom = jnp.zeros((24, 384), jnp.float32), jnp.zeros((24, 384), jnp.float32)
    wide_lane = lax.broadcasted_iota(jnp.int32, (24, 384), 1)
    for b in range(8):
        arrived(block_in.at[b], recv4.at[b])
        both = jnp.concatenate([block_in[b], jnp.zeros((24, 256), jnp.float32)], axis=1)
        above = jnp.where(wide_lane < 48, both, 0.0)
        top = top + (pltpu.roll(above, 48 * b, 1) if b else above)
        below = both - above
        bottom = bottom + (pltpu.roll(below, (48 * b + 336) % 384, 1) if b != 1 else below)
    rows_out[0:24] = cycle[0:24] + top
    rows_out[24:48] = cycle[24:48] + bottom

    columns = pl.ds(pl.multiple_of(384 * rep, 128), 384)
    for c in range(2):
        to = (2 * (8 * layer + 4 * core + pan) + c, (owner + pan) % 4, rep)
        send_or_keep(rows_out.at[24 * c:24 * (c + 1)], out_ref.at[owner, :, columns], send5.at[c], recv5.at[owner // 4], to)

    def place(half, i, j):
        x, y = (pan + j, rep + i) if half == 0 else (pan + i, rep + j)
        return x % 4, y % 4

    def rows(half, i, j):
        x, y = place(half, i, j)
        return out_ref.at[(x + 4 - z % 4) % 4 + 4 * half, :, pl.ds(pl.multiple_of(384 * y, 128), 384)]

    def to_neighbours(half, i):
        here = rows(half, i, 0)
        for way in (1, 3):
            send(here, here, send7.at[half, way // 2, i], recv7.at[half, way // 2, i], (wide,) + place(half, 0, way))

    for half in range(2):
        here = rows(half, 0, 0)
        arrived(here, recv5.at[half])
        for i in (1, 3, 2):
            send(here, here, send6.at[half, i], recv6.at[half, 4 - i], (wide,) + place(half, i, 0))
        to_neighbours(half, 0)
    for i in (1, 3, 2):
        for half in range(2):
            arrived(rows(half, i, 0), recv6.at[half, i])
            to_neighbours(half, i)
    for i in (0, 1, 3, 2):
        for half in range(2):
            arrived(rows(half, i, 3), recv7.at[half, 0, i])
            arrived(rows(half, i, 1), recv7.at[half, 1, i])
            come, go = (1, 3) if i < 2 else (3, 1)
            here = rows(half, i, come)
            send(here, here, send8.at[half, i], recv8.at[half, i], (wide,) + place(half, 0, go))
    for i in (0, 1, 3, 2):
        for half in range(2):
            arrived(rows(half, i, 2), recv8.at[half, i])

    for args in sent:
        remote(*args).wait_send()
    for args in sent_or_kept:
        finish_send(*args)


def shards(amplitudes, integrals, pair_energies, block_sizes):
    vmem = pl.BlockSpec(memory_space=pltpu.VMEM)
    hbm = pl.BlockSpec(memory_space=pltpu.HBM)
    dma = pltpu.SemaphoreType.DMA
    residual = pl.pallas_call(
        cycle_kernel,
        out_shape=jax.ShapeDtypeStruct((8, 24, 1536), jnp.float32),
        in_specs=[pl.BlockSpec(memory_space=pltpu.SMEM), hbm, hbm],
        out_specs=vmem,
        scratch_shapes=[
            pltpu.VMEM((8, 24, 96), jnp.float32),
            pltpu.VMEM((8, 24, 96), jnp.float32),
            pltpu.VMEM((2, 8, 18, 128), jnp.float32),
            pltpu.VMEM((4, 8, 18, 128), jnp.float32),
            pltpu.VMEM((2, 4, 8, 18, 128), jnp.float32),
            pltpu.VMEM((4, 192, 128), jnp.float32),
            pltpu.VMEM((2, 4, 192, 128), jnp.float32),
            pltpu.VMEM((192, 384), jnp.float32),
            pltpu.VMEM((4, 48, 384), jnp.float32),
            pltpu.VMEM((8, 24, 128), jnp.float32),
            pltpu.VMEM((8, 24, 128), jnp.float32),
            pltpu.VMEM((48, 384), jnp.float32),
            dma((2,)), dma((2, 8)), dma((2, 8)),
            dma((4, 4)), dma((4, 4)), dma((4, 4)), dma((4, 4)), dma((4, 4)), dma((4, 4)),
            dma((4,)), dma((4,)), dma((8,)), dma((8,)), dma((2,)), dma((2,)),
            dma((2, 4)), dma((2, 4)), dma((2, 2, 4)), dma((2, 2, 4)), dma((2, 4)), dma((2, 4)),
        ],
        compiler_params=pltpu.CompilerParams(collective_id=0, has_side_effects=True, vmem_limit_bytes=24 * 1024 * 1024),
        cost_estimate=pl.CostEstimate(flops=60_000_000, bytes_accessed=2_000_000, transcendentals=0),
    )(block_sizes, amplitudes, jnp.swapaxes(integrals, 1, 2))
    row_start = lax.axis_index("wide") * 24
    energy_rows = lax.dynamic_slice_in_dim(pair_energies, row_start, 24, 1)
    update = -residual / (energy_rows[:, :, None] + pair_energies[:, None, :])
    return (residual, update)


def solution(mesh):
    in_specs = (P(None, "wide", ("pan", "rep")), P(None, ("pan", "rep"), "wide"), P(), P())
    out_specs = (P(None, "wide", None), P(None, "wide", None))
    return jax.shard_map(shards, mesh=mesh, in_specs=in_specs, out_specs=out_specs, check_vma=False)
```

```python
import jax
import jax.numpy as jnp
from jax import lax
from jax.experimental import pallas as pl
from jax.experimental.pallas import tpu as pltpu
from jax.sharding import PartitionSpec as P

MESH = pl.DeviceIdType.MESH


def cycle_kernel(
    sizes_hbm, amp_hbm, int_hbm, out_ref,
    sizes_ref, amp_ref, int_ref, stage, amp_packed, int_packed, amp_all, int_all, part, parts, block_out, block_in, rows_out,
    load, send1, recv1, send_a, recv_a, send_b, recv_b, send_c, recv_c,
    send3, recv3, send4, recv4, send5, recv5, send6, recv6, send7, recv7, send8, recv8,
):
    wide, pan, rep = lax.axis_index("wide"), lax.axis_index("pan"), lax.axis_index("rep")
    z, core = wide // 2, wide % 2
    owner, layer = z // 4, z % 4
    band, rank = z // 8, z % 8

    def device(w, x, y):
        return {"wide": w, "pan": x, "rep": y}

    def remote(src, dst, ssem, rsem, to):
        return pltpu.make_async_remote_copy(
            src_ref=src, dst_ref=dst, send_sem=ssem, recv_sem=rsem,
            device_id=device(*to), device_id_type=MESH,
        )

    def is_me(to):
        return (to[0] == wide) & (to[1] == pan) & (to[2] == rep)

    def start(src, dst, ssem, rsem, to):
        me = is_me(to)

        @pl.when(me)
        def _():
            pltpu.make_async_copy(src, dst, rsem).start()

        @pl.when(jnp.logical_not(me))
        def _():
            remote(src, dst, ssem, rsem, to).start()

    def finish_send(src, dst, ssem, rsem, to):
        @pl.when(jnp.logical_not(is_me(to)))
        def _():
            remote(src, dst, ssem, rsem, to).wait_send()

    def arrived(dst, rsem):
        pltpu.make_async_copy(dst, dst, rsem).wait()

    sent, sent_or_kept = [], []

    def send(*args):
        sent.append(args)
        remote(*args).start()

    def send_or_keep(*args):
        sent_or_kept.append(args)
        start(*args)

    loads = [
        pltpu.make_async_copy(amp_hbm, amp_ref, load.at[0]),
        pltpu.make_async_copy(int_hbm, int_ref, load.at[1]),
        pltpu.make_async_copy(sizes_hbm, sizes_ref, load.at[2]),
    ]
    for copy in loads:
        copy.start()

    def block_at(x, at, far):
        one = (x + 4 - at % 4) % 4
        off = (4 * one + 2 + 32 - at) % 32
        return (one + 4 * (((off + 7) % 32) // 16) + 4 * far) % 8

    callers = [(2 * (8 * layer + 4 * core + i // 2) + i % 2, pan, rep) for i in range(8)]
    callers += [(2 * (8 * rep + 4 * core + i // 2) + i % 2, pan, layer) for i in range(8)]
    callers += [(wide, pan, (rep + step) % 4) for step in range(1, 4)]
    callers += [(wide, (pan + step) % 4, rep) for step in range(1, 4)]
    callers += [(2 * z + 1 - core, pan, rep)]
    callers += [(2 * (4 * owner + (layer + step) % 4) + core, pan, rep) for step in range(1, 4)]
    callers += [(2 * (4 * owner + rep) + b // 4, b % 4, layer) for b in range(8)]
    callers += [(2 * (4 * block_at(pan, z, far) + band) + rank // 4, z % 4, rep) for far in range(2)]
    barrier = pltpu.get_barrier_semaphore()
    for to in callers:
        pl.semaphore_signal(barrier, inc=1, device_id=device(*to), device_id_type=MESH)

    row_at = wide * 24 + lax.broadcasted_iota(jnp.int32, (24, 128), 0)
    lane = lax.broadcasted_iota(jnp.int32, (24, 128), 1)
    sum_at = (pan * 4 + rep) * 96 + lane
    lane8 = lane[0:8]
    for copy in loads:
        copy.wait()
    for h in range(8):
        live = (row_at < sizes_ref[h]) & (sum_at < sizes_ref[h]) & (lane < 96)
        for side, ref in enumerate((amp_ref, int_ref)):
            value = jnp.concatenate([ref[h], jnp.zeros((24, 32), jnp.float32)], axis=1)
            value = jnp.where(live, value, 0.0)
            last = value[16:24]
            stage[side, h, 0:8] = jnp.where(lane8 < 96, value[0:8], pltpu.roll(last, 96, 1))
            stage[side, h, 8:16] = jnp.where(lane8 < 96, value[8:16], pltpu.roll(last, 64, 1))
            pairs = pltpu.roll(last, 64, 1)
            pairs = jnp.where(lane8 < 32, pairs, pltpu.roll(pltpu.roll(last, 96, 1), 6, 0))
            pairs = jnp.where(lane8 < 64, pairs, pltpu.roll(last, 4, 0))
            pairs = jnp.where(lane8 < 96, pairs, pltpu.roll(pltpu.roll(last, 32, 1), 2, 0))
            stage[side, h, 16:18] = pairs[0:2]
    pl.semaphore_wait(barrier, len(callers))

    slot1 = (rank % 4) * 2 + core
    for step in (4, 3, 5, 2, 6, 1, 7, 0):
        h = (owner + step) % 8
        to = (2 * (4 * h + band) + rank // 4, pan, rep)
        send_or_keep(stage.at[0, h], amp_packed.at[rep, slot1], send1.at[0, step], recv1.at[0, slot1], to)
        to = (2 * (4 * h + rep) + rank // 4, pan, band)
        send_or_keep(stage.at[1, h], int_packed.at[rank // 4, rep, slot1], send1.at[1, step], recv1.at[1, slot1], to)

    sibling = (2 * z + 1 - core, pan, rep)
    for pair in range(4):
        two = slice(2 * pair, 2 * pair + 2)
        for i in (2 * pair, 2 * pair + 1):
            arrived(amp_packed.at[rep, i], recv1.at[0, i])
        here = amp_packed.at[rep, two]
        for step in range(1, 4):
            send(here, here, send_a.at[pair, step], recv_a.at[pair, rep], (wide, pan, (rep + step) % 4))
        for i in (2 * pair, 2 * pair + 1):
            arrived(int_packed.at[core, layer, i], recv1.at[1, i])
        here = int_packed.at[core, layer, two]
        for step in range(1, 4):
            to = (2 * (4 * owner + (layer + step) % 4) + core, pan, rep)
            send(here, here, send_b.at[pair, step], recv_b.at[pair, layer], to)
        send(here, here, send_c.at[pair, 0], recv_c.at[pair, layer], sibling)

    def unpack(packed, whole, index, mask):
        for i in range(8):
            one, two = packed[index + (i, slice(0, 8))], packed[index + (i, slice(8, 16))]
            tail = jnp.concatenate([packed[index + (i, slice(16, 18))], jnp.zeros((6, 128), jnp.float32)], axis=0)
            last = pltpu.roll(tail, 64, 1) + pltpu.roll(pltpu.roll(tail, 32, 1), 2, 0)
            last = last + pltpu.roll(tail, 4, 0) + pltpu.roll(pltpu.roll(tail, 96, 1), 6, 0)
            last = jnp.where(lane8 < 64, pltpu.roll(two, 64, 1), last)
            last = jnp.where(lane8 < 32, pltpu.roll(one, 32, 1), last)
            for row, value in ((0, one), (8, two), (16, last)):
                whole[index + (slice(24 * i + row, 24 * i + row + 8),)] = jnp.where(lane8 < 96, value, 0.0) if mask else value

    unpack(amp_packed, amp_all, (rep,), True)
    unpack(int_packed, int_all, (core, layer), False)
    for step in (1, 3, 2):
        y, l = (rep + step) % 4, (layer + step) % 4
        for pair in range(4):
            two = slice(2 * pair, 2 * pair + 2)
            arrived(int_packed.at[core, l, two], recv_b.at[pair, l])
            here = int_packed.at[core, l, two]
            send(here, here, send_c.at[pair, step], recv_c.at[pair, l], sibling)
        unpack(int_packed, int_all, (core, l), False)
        for pair in range(4):
            arrived(amp_packed.at[y, 2 * pair:2 * pair + 2], recv_a.at[pair, y])
        unpack(amp_packed, amp_all, (y,), True)
    for step in (0, 1, 3, 2):
        l = (layer + step) % 4
        for pair in range(4):
            arrived(int_packed.at[1 - core, l, 2 * pair:2 * pair + 2], recv_c.at[pair, l])
        unpack(int_packed, int_all, (1 - core, l), False)

    for side in range(2):
        total = jnp.zeros((192, 192), jnp.float32)
        for y in range(4):
            total = total + lax.dot_general(
                amp_all[y], int_all[side, y],
                (((1,), (1,)), ((), ())), precision=lax.Precision.HIGHEST, preferred_element_type=jnp.float32,
            )
        part[:, 192 * side:192 * (side + 1)] = total
    for step in range(1, 4):
        x = (pan + step) % 4
        rows = part.at[pl.ds(pl.multiple_of(48 * x, 8), 48)]
        send(rows, parts.at[pan], send3.at[step], recv3.at[pan], (wide, x, rep))
    parts[pan] = part[pl.ds(pl.multiple_of(48 * pan, 8), 48)]
    for step in range(1, 4):
        x = (pan + step) % 4
        arrived(parts.at[x], recv3.at[x])
    cycle = parts[0] + parts[1] + parts[2] + parts[3]

    flipped = jnp.concatenate([cycle, jnp.zeros((80, 384), jnp.float32)], axis=0).T.reshape(8, 2, 24, 128)
    right = pltpu.roll(flipped[:, 1].reshape(192, 128), 48, 1)
    block_out[...] = flipped[:, 0] + right.reshape(8, 24, 128)
    mine = 4 * core + pan
    for step in range(8):
        b = (mine + step) % 8
        to = (2 * (4 * owner + rep) + b // 4, b % 4, layer)
        send_or_keep(block_out.at[b], block_in.at[mine], send4.at[step], recv4.at[mine], to)
    top, bottom = jnp.zeros((24, 384), jnp.float32), jnp.zeros((24, 384), jnp.float32)
    wide_lane = lax.broadcasted_iota(jnp.int32, (24, 384), 1)
    for b in range(8):
        arrived(block_in.at[b], recv4.at[b])
        both = jnp.concatenate([block_in[b], jnp.zeros((24, 256), jnp.float32)], axis=1)
        above = jnp.where(wide_lane < 48, both, 0.0)
        top = top + (pltpu.roll(above, 48 * b, 1) if b else above)
        below = both - above
        bottom = bottom + (pltpu.roll(below, (48 * b + 336) % 384, 1) if b != 1 else below)
    rows_out[0:24] = -(cycle[0:24] + top)
    rows_out[24:48] = -(cycle[24:48] + bottom)

    columns = pl.ds(pl.multiple_of(384 * rep, 128), 384)
    goal = 8 * layer + 4 * core + pan
    column = (owner + pan) % 4
    far = ((owner + 8 - block_at(column, goal, 0)) % 8) // 4
    for c in range(2):
        to = (2 * goal + c, column, rep)
        send_or_keep(rows_out.at[24 * c:24 * (c + 1)], out_ref.at[owner, :, columns], send5.at[c], recv5.at[far], to)

    def place(half, i, j):
        x, y = (pan + j, rep + i) if half == 0 else (pan + i, rep + j)
        return x % 4, y % 4

    def rows(half, i, j):
        x, y = place(half, i, j)
        return out_ref.at[block_at(x, z, half), :, pl.ds(pl.multiple_of(384 * y, 128), 384)]

    def to_neighbours(half, i):
        here = rows(half, i, 0)
        for way in (1, 3):
            send(here, here, send7.at[half, way // 2, i], recv7.at[half, way // 2, i], (wide,) + place(half, 0, way))

    for half in range(2):
        here = rows(half, 0, 0)
        arrived(here, recv5.at[half])
        for i in (1, 3, 2):
            send(here, here, send6.at[half, i], recv6.at[half, 4 - i], (wide,) + place(half, i, 0))
        to_neighbours(half, 0)
        for i in (1, 3, 2):
            arrived(rows(half, i, 0), recv6.at[half, i])
            to_neighbours(half, i)
        for i in (0, 1, 3, 2):
            come, go = (1, 3) if i < 2 else (3, 1)
            here = rows(half, i, come)
            arrived(here, recv7.at[half, 1 if i < 2 else 0, i])
            send(here, here, send8.at[half, i], recv8.at[half, i], (wide,) + place(half, 0, go))
    for half in range(2):
        for i in range(4):
            arrived(rows(half, i, 3 if i < 2 else 1), recv7.at[half, 0 if i < 2 else 1, i])
            arrived(rows(half, i, 2), recv8.at[half, i])

    for args in sent:
        remote(*args).wait_send()
    for args in sent_or_kept:
        finish_send(*args)


def shards(amplitudes, integrals, pair_energies, block_sizes):
    vmem = pl.BlockSpec(memory_space=pltpu.VMEM)
    hbm = pl.BlockSpec(memory_space=pltpu.HBM)
    dma = pltpu.SemaphoreType.DMA
    negated = pl.pallas_call(
        cycle_kernel,
        out_shape=jax.ShapeDtypeStruct((8, 24, 1536), jnp.float32),
        in_specs=[hbm, hbm, hbm],
        out_specs=vmem,
        scratch_shapes=[
            pltpu.SMEM((8,), jnp.int32),
            pltpu.VMEM((8, 24, 96), jnp.float32),
            pltpu.VMEM((8, 24, 96), jnp.float32),
            pltpu.VMEM((2, 8, 18, 128), jnp.float32),
            pltpu.VMEM((4, 8, 18, 128), jnp.float32),
            pltpu.VMEM((2, 4, 8, 18, 128), jnp.float32),
            pltpu.VMEM((4, 192, 128), jnp.float32),
            pltpu.VMEM((2, 4, 192, 128), jnp.float32),
            pltpu.VMEM((192, 384), jnp.float32),
            pltpu.VMEM((4, 48, 384), jnp.float32),
            pltpu.VMEM((8, 24, 128), jnp.float32),
            pltpu.VMEM((8, 24, 128), jnp.float32),
            pltpu.VMEM((48, 384), jnp.float32),
            dma((3,)), dma((2, 8)), dma((2, 8)),
            dma((4, 4)), dma((4, 4)), dma((4, 4)), dma((4, 4)), dma((4, 4)), dma((4, 4)),
            dma((4,)), dma((4,)), dma((8,)), dma((8,)), dma((2,)), dma((2,)),
            dma((2, 4)), dma((2, 4)), dma((2, 2, 4)), dma((2, 2, 4)), dma((2, 4)), dma((2, 4)),
        ],
        compiler_params=pltpu.CompilerParams(collective_id=0, has_side_effects=True, vmem_limit_bytes=24 * 1024 * 1024),
        cost_estimate=pl.CostEstimate(flops=60_000_000, bytes_accessed=2_000_000, transcendentals=0),
    )(*(pltpu.with_memory_space_constraint(operand, pltpu.HBM) for operand in (block_sizes, amplitudes, jnp.swapaxes(integrals, 1, 2))))
    row_start = lax.axis_index("wide") * 24
    energy_rows = lax.dynamic_slice_in_dim(pair_energies, row_start, 24, 1)
    update = negated / (energy_rows[:, :, None] + pair_energies[:, None, :])
    return (-negated, update)


def solution(mesh):
    in_specs = (P(None, "wide", ("pan", "rep")), P(None, ("pan", "rep"), "wide"), P(), P())
    out_specs = (P(None, "wide", None), P(None, "wide", None))
    return jax.shard_map(shards, mesh=mesh, in_specs=in_specs, out_specs=out_specs, check_vma=False)
```

```python
import jax
import jax.numpy as jnp
from jax import lax
from jax.experimental import pallas as pl
from jax.experimental.pallas import tpu as pltpu
from jax.sharding import PartitionSpec as P

MESH = pl.DeviceIdType.MESH


def cycle_kernel(
    sizes_hbm, amp_hbm, int_hbm, out_ref,
    sizes_ref, amp_ref, int_ref, stage, amp_packed, int_packed, amp_all, int_all, part, parts, block_out, block_in, rows_out,
    load, send1, recv1, send_a, recv_a, send_b, recv_b, send_c, recv_c,
    send3, recv3, send4, recv4, send5, recv5, send6, recv6, send7, recv7, send8, recv8,
):
    wide, pan, rep = lax.axis_index("wide"), lax.axis_index("pan"), lax.axis_index("rep")
    z, core = wide // 2, wide % 2
    owner, layer = z // 4, z % 4
    band, rank = z // 8, z % 8

    def device(w, x, y):
        return {"wide": w, "pan": x, "rep": y}

    def remote(src, dst, ssem, rsem, to):
        return pltpu.make_async_remote_copy(
            src_ref=src, dst_ref=dst, send_sem=ssem, recv_sem=rsem,
            device_id=device(*to), device_id_type=MESH,
        )

    def is_me(to):
        return (to[0] == wide) & (to[1] == pan) & (to[2] == rep)

    def start(src, dst, ssem, rsem, to):
        me = is_me(to)

        @pl.when(me)
        def _():
            pltpu.make_async_copy(src, dst, rsem).start()

        @pl.when(jnp.logical_not(me))
        def _():
            remote(src, dst, ssem, rsem, to).start()

    def finish_send(src, dst, ssem, rsem, to):
        @pl.when(jnp.logical_not(is_me(to)))
        def _():
            remote(src, dst, ssem, rsem, to).wait_send()

    def arrived(dst, rsem):
        pltpu.make_async_copy(dst, dst, rsem).wait()

    sent, sent_or_kept = [], []

    def send(*args):
        sent.append(args)
        remote(*args).start()

    def send_or_keep(*args):
        sent_or_kept.append(args)
        start(*args)

    loads = [
        pltpu.make_async_copy(amp_hbm, amp_ref, load.at[0]),
        pltpu.make_async_copy(int_hbm, int_ref, load.at[1]),
        pltpu.make_async_copy(sizes_hbm, sizes_ref, load.at[2]),
    ]
    for copy in loads:
        copy.start()

    def block_at(x, at, far):
        one = (x + 4 - at % 4) % 4
        off = (4 * one + 2 + 32 - at) % 32
        return (one + 4 * (((off + 7) % 32) // 16) + 4 * far) % 8

    callers = [(2 * (8 * layer + 4 * core + i // 2) + i % 2, pan, rep) for i in range(8)]
    callers += [(2 * (8 * rep + 4 * core + i // 2) + i % 2, pan, layer) for i in range(8)]
    callers += [(wide, pan, (rep + step) % 4) for step in range(1, 4)]
    callers += [(wide, (pan + step) % 4, rep) for step in range(1, 4)]
    callers += [(2 * z + 1 - core, pan, rep)]
    callers += [(2 * (4 * owner + (layer + step) % 4) + core, pan, rep) for step in range(1, 4)]
    callers += [(2 * (4 * owner + rep) + b // 4, b % 4, layer) for b in range(8)]
    callers += [(2 * (4 * block_at(pan, z, far) + band) + rank // 4, z % 4, rep) for far in range(2)]
    barrier = pltpu.get_barrier_semaphore()
    for to in callers:
        pl.semaphore_signal(barrier, inc=1, device_id=device(*to), device_id_type=MESH)

    row_at = wide * 24 + lax.broadcasted_iota(jnp.int32, (24, 128), 0)
    lane = lax.broadcasted_iota(jnp.int32, (24, 128), 1)
    sum_at = (pan * 4 + rep) * 96 + lane
    lane8 = lane[0:8]

    def pack(value):
        last = value[16:24]
        pairs = jnp.where(lane8 < 32, pltpu.roll(last, 64, 1), pltpu.roll(pltpu.roll(last, 96, 1), 6, 0))
        pairs = jnp.where(lane8 < 64, pairs, pltpu.roll(last, 4, 0))
        pairs = jnp.where(lane8 < 96, pairs, pltpu.roll(pltpu.roll(last, 32, 1), 2, 0))
        return (
            jnp.where(lane8 < 96, value[0:8], pltpu.roll(last, 96, 1)),
            jnp.where(lane8 < 96, value[8:16], pltpu.roll(last, 64, 1)),
            pairs[0:2],
        )

    def unpack(one, two, tail):
        tail = jnp.concatenate([tail, jnp.zeros((6, 128), jnp.float32)], axis=0)
        last = pltpu.roll(tail, 64, 1) + pltpu.roll(pltpu.roll(tail, 32, 1), 2, 0)
        last = last + pltpu.roll(tail, 4, 0) + pltpu.roll(pltpu.roll(tail, 96, 1), 6, 0)
        last = jnp.where(lane8 < 64, pltpu.roll(two, 64, 1), last)
        return one, two, jnp.where(lane8 < 32, pltpu.roll(one, 32, 1), last)

    for copy in loads:
        copy.wait()
    for h in range(8):
        live = (row_at < sizes_ref[h]) & (sum_at < sizes_ref[h]) & (lane < 96)
        for side, ref in enumerate((amp_ref, int_ref)):
            value = jnp.concatenate([ref[h], jnp.zeros((24, 32), jnp.float32)], axis=1)
            value = jnp.where(live, value, 0.0)
            for row, part_of in zip((0, 8, 16), pack(value)):
                stage[side, h, row:row + part_of.shape[0]] = part_of
    pl.semaphore_wait(barrier, len(callers))

    slot1 = (rank % 4) * 2 + core
    for step in (4, 3, 5, 2, 6, 1, 7, 0):
        h = (owner + step) % 8
        to = (2 * (4 * h + band) + rank // 4, pan, rep)
        send_or_keep(stage.at[0, h], amp_packed.at[rep, slot1], send1.at[0, step], recv1.at[0, slot1], to)
        to = (2 * (4 * h + rep) + rank // 4, pan, band)
        send_or_keep(stage.at[1, h], int_packed.at[rank // 4, rep, slot1], send1.at[1, step], recv1.at[1, slot1], to)

    sibling = (2 * z + 1 - core, pan, rep)
    for pair in range(4):
        two = slice(2 * pair, 2 * pair + 2)
        for i in (2 * pair, 2 * pair + 1):
            arrived(amp_packed.at[rep, i], recv1.at[0, i])
        here = amp_packed.at[rep, two]
        for step in range(1, 4):
            send(here, here, send_a.at[pair, step], recv_a.at[pair, rep], (wide, pan, (rep + step) % 4))
        for i in (2 * pair, 2 * pair + 1):
            arrived(int_packed.at[core, layer, i], recv1.at[1, i])
        here = int_packed.at[core, layer, two]
        for step in range(1, 4):
            to = (2 * (4 * owner + (layer + step) % 4) + core, pan, rep)
            send(here, here, send_b.at[pair, step], recv_b.at[pair, layer], to)
        send(here, here, send_c.at[pair, 0], recv_c.at[pair, layer], sibling)

    def spread(packed, whole, index, mask):
        for i in range(8):
            values = unpack(*(packed[index + (i, slice(*rows))] for rows in ((0, 8), (8, 16), (16, 18))))
            for row, value in zip((0, 8, 16), values):
                whole[index + (slice(24 * i + row, 24 * i + row + 8),)] = jnp.where(lane8 < 96, value, 0.0) if mask else value

    spread(amp_packed, amp_all, (rep,), True)
    spread(int_packed, int_all, (core, layer), False)
    for step in (1, 3, 2):
        y, l = (rep + step) % 4, (layer + step) % 4
        for pair in range(4):
            two = slice(2 * pair, 2 * pair + 2)
            arrived(int_packed.at[core, l, two], recv_b.at[pair, l])
            here = int_packed.at[core, l, two]
            send(here, here, send_c.at[pair, step], recv_c.at[pair, l], sibling)
        spread(int_packed, int_all, (core, l), False)
        for pair in range(4):
            arrived(amp_packed.at[y, 2 * pair:2 * pair + 2], recv_a.at[pair, y])
        spread(amp_packed, amp_all, (y,), True)
    for step in (0, 1, 3, 2):
        l = (layer + step) % 4
        for pair in range(4):
            arrived(int_packed.at[1 - core, l, 2 * pair:2 * pair + 2], recv_c.at[pair, l])
        spread(int_packed, int_all, (1 - core, l), False)

    for side in range(2):
        total = jnp.zeros((192, 192), jnp.float32)
        for y in range(4):
            total = total + lax.dot_general(
                amp_all[y], int_all[side, y],
                (((1,), (1,)), ((), ())), precision=lax.Precision.HIGHEST, preferred_element_type=jnp.float32,
            )
        part[:, 192 * side:192 * (side + 1)] = total
    for step in range(1, 4):
        x = (pan + step) % 4
        rows = part.at[pl.ds(pl.multiple_of(48 * x, 8), 48)]
        send(rows, parts.at[pan], send3.at[step], recv3.at[pan], (wide, x, rep))
    parts[pan] = part[pl.ds(pl.multiple_of(48 * pan, 8), 48)]
    for step in range(1, 4):
        x = (pan + step) % 4
        arrived(parts.at[x], recv3.at[x])
    cycle = parts[0] + parts[1] + parts[2] + parts[3]

    flipped = jnp.concatenate([cycle, jnp.zeros((80, 384), jnp.float32)], axis=0).T.reshape(8, 2, 24, 128)
    right = pltpu.roll(flipped[:, 1].reshape(192, 128), 48, 1)
    paired = flipped[:, 0] + right.reshape(8, 24, 128)
    for b in range(8):
        for row, part_of in zip((0, 8, 16), pack(paired[b])):
            block_out[b, row:row + part_of.shape[0]] = part_of
    mine = 4 * core + pan
    for step in range(8):
        b = (mine + step) % 8
        to = (2 * (4 * owner + rep) + b // 4, b % 4, layer)
        send_or_keep(block_out.at[b], block_in.at[mine], send4.at[step], recv4.at[mine], to)
    top, bottom = jnp.zeros((24, 384), jnp.float32), jnp.zeros((24, 384), jnp.float32)
    wide_lane = lax.broadcasted_iota(jnp.int32, (24, 384), 1)
    for b in range(8):
        arrived(block_in.at[b], recv4.at[b])
        both = jnp.concatenate(unpack(block_in[b, 0:8], block_in[b, 8:16], block_in[b, 16:18]), axis=0)
        both = jnp.concatenate([jnp.where(lane < 96, both, 0.0), jnp.zeros((24, 256), jnp.float32)], axis=1)
        above = jnp.where(wide_lane < 48, both, 0.0)
        top = top + (pltpu.roll(above, 48 * b, 1) if b else above)
        below = both - above
        bottom = bottom + (pltpu.roll(below, (48 * b + 336) % 384, 1) if b != 1 else below)
    rows_out[0:24] = -(cycle[0:24] + top)
    rows_out[24:48] = -(cycle[24:48] + bottom)

    columns = pl.ds(pl.multiple_of(384 * rep, 128), 384)
    goal = 8 * layer + 4 * core + pan
    column = (owner + pan) % 4
    far = ((owner + 8 - block_at(column, goal, 0)) % 8) // 4
    for c in range(2):
        to = (2 * goal + c, column, rep)
        send_or_keep(rows_out.at[24 * c:24 * (c + 1)], out_ref.at[owner, :, columns], send5.at[c], recv5.at[far], to)

    def place(i, j):
        return (pan + i * core + j * (1 - core)) % 4, (rep + i * (1 - core) + j * core) % 4

    def rows(half, i, j):
        x, y = place(i, j)
        return out_ref.at[block_at(x, z, half), :, pl.ds(pl.multiple_of(384 * y, 128), 384)]

    def to_neighbours(half, i):
        here = rows(half, i, 0)
        if i == 2:
            send(here, here, send8.at[half, 2], recv8.at[half, 2], (wide,) + place(0, 2))
        for way in (1, 3):
            send(here, here, send7.at[half, way // 2, i], recv7.at[half, way // 2, i], (wide,) + place(0, way))

    for half in range(2):
        here = rows(half, 0, 0)
        arrived(here, recv5.at[half])
        for i in (2, 1, 3):
            send(here, here, send6.at[half, i], recv6.at[half, 4 - i], (wide,) + place(i, 0))
        to_neighbours(half, 0)
        for i in (1, 3, 2):
            arrived(rows(half, i, 0), recv6.at[half, i])
            to_neighbours(half, i)
        for i in (0, 1, 3):
            come, go = (1, 3) if i < 2 else (3, 1)
            here = rows(half, i, come)
            arrived(here, recv7.at[half, 1 if i < 2 else 0, i])
            send(here, here, send8.at[half, i], recv8.at[half, i], (wide,) + place(0, go))
    for half in range(2):
        for i in range(4):
            if i != 2:
                arrived(rows(half, i, 3 if i < 2 else 1), recv7.at[half, 0 if i < 2 else 1, i])
            else:
                arrived(rows(half, i, 3), recv7.at[half, 0, i])
                arrived(rows(half, i, 1), recv7.at[half, 1, i])
            arrived(rows(half, i, 2), recv8.at[half, i])

    for args in sent:
        remote(*args).wait_send()
    for args in sent_or_kept:
        finish_send(*args)


def shards(amplitudes, integrals, pair_energies, block_sizes):
    vmem = pl.BlockSpec(memory_space=pltpu.VMEM)
    hbm = pl.BlockSpec(memory_space=pltpu.HBM)
    dma = pltpu.SemaphoreType.DMA
    negated = pl.pallas_call(
        cycle_kernel,
        out_shape=jax.ShapeDtypeStruct((8, 24, 1536), jnp.float32),
        in_specs=[hbm, hbm, hbm],
        out_specs=vmem,
        scratch_shapes=[
            pltpu.SMEM((8,), jnp.int32),
            pltpu.VMEM((8, 24, 96), jnp.float32),
            pltpu.VMEM((8, 24, 96), jnp.float32),
            pltpu.VMEM((2, 8, 18, 128), jnp.float32),
            pltpu.VMEM((4, 8, 18, 128), jnp.float32),
            pltpu.VMEM((2, 4, 8, 18, 128), jnp.float32),
            pltpu.VMEM((4, 192, 128), jnp.float32),
            pltpu.VMEM((2, 4, 192, 128), jnp.float32),
            pltpu.VMEM((192, 384), jnp.float32),
            pltpu.VMEM((4, 48, 384), jnp.float32),
            pltpu.VMEM((8, 18, 128), jnp.float32),
            pltpu.VMEM((8, 18, 128), jnp.float32),
            pltpu.VMEM((48, 384), jnp.float32),
            dma((3,)), dma((2, 8)), dma((2, 8)),
            dma((4, 4)), dma((4, 4)), dma((4, 4)), dma((4, 4)), dma((4, 4)), dma((4, 4)),
            dma((4,)), dma((4,)), dma((8,)), dma((8,)), dma((2,)), dma((2,)),
            dma((2, 4)), dma((2, 4)), dma((2, 2, 4)), dma((2, 2, 4)), dma((2, 4)), dma((2, 4)),
        ],
        compiler_params=pltpu.CompilerParams(collective_id=0, has_side_effects=True, vmem_limit_bytes=24 * 1024 * 1024),
        cost_estimate=pl.CostEstimate(flops=60_000_000, bytes_accessed=2_000_000, transcendentals=0),
    )(*(pltpu.with_memory_space_constraint(operand, pltpu.HBM) for operand in (block_sizes, amplitudes, jnp.swapaxes(integrals, 1, 2))))
    negated, pair_energies = lax.optimization_barrier((negated, pair_energies))
    row_start = lax.axis_index("wide") * 24
    energy_rows = lax.dynamic_slice_in_dim(pair_energies, row_start, 24, 1)
    update = negated / (energy_rows[:, :, None] + pair_energies[:, None, :])
    return (-negated, update)


def solution(mesh):
    in_specs = (P(None, "wide", ("pan", "rep")), P(None, ("pan", "rep"), "wide"), P(), P())
    out_specs = (P(None, "wide", None), P(None, "wide", None))
    return jax.shard_map(shards, mesh=mesh, in_specs=in_specs, out_specs=out_specs, check_vma=False)
```

```python
import jax
import jax.numpy as jnp
from jax import lax
from jax.experimental import pallas as pl
from jax.experimental.pallas import tpu as pltpu
from jax.sharding import PartitionSpec as P

MESH = pl.DeviceIdType.MESH


def cycle_kernel(
    sizes_hbm, amp_hbm, int_hbm, out_ref,
    sizes_ref, amp_ref, int_ref, stage, amp_packed, int_packed, amp_all, int_all, part, parts, block_out, block_in, rows_out,
    load, send1, recv1, send_a, recv_a, send_b, recv_b, send_c, recv_c,
    send3, recv3, send4, recv4, send5, recv5, send6, recv6, send7, recv7, send8, recv8,
):
    wide, pan, rep = lax.axis_index("wide"), lax.axis_index("pan"), lax.axis_index("rep")
    z, core = wide // 2, wide % 2
    owner, layer = z // 4, z % 4
    band, rank = z // 8, z % 8

    def device(w, x, y):
        return {"wide": w, "pan": x, "rep": y}

    def remote(src, dst, ssem, rsem, to):
        return pltpu.make_async_remote_copy(
            src_ref=src, dst_ref=dst, send_sem=ssem, recv_sem=rsem,
            device_id=device(*to), device_id_type=MESH,
        )

    def is_me(to):
        return (to[0] == wide) & (to[1] == pan) & (to[2] == rep)

    def start(src, dst, ssem, rsem, to):
        me = is_me(to)

        @pl.when(me)
        def _():
            pltpu.make_async_copy(src, dst, rsem).start()

        @pl.when(jnp.logical_not(me))
        def _():
            remote(src, dst, ssem, rsem, to).start()

    def finish_send(src, dst, ssem, rsem, to):
        @pl.when(jnp.logical_not(is_me(to)))
        def _():
            remote(src, dst, ssem, rsem, to).wait_send()

    def arrived(dst, rsem):
        pltpu.make_async_copy(dst, dst, rsem).wait()

    sent, sent_or_kept = [], []

    def send(*args):
        sent.append(args)
        remote(*args).start()

    def send_or_keep(*args):
        sent_or_kept.append(args)
        start(*args)

    loads = [
        pltpu.make_async_copy(amp_hbm, amp_ref, load.at[0]),
        pltpu.make_async_copy(int_hbm, int_ref, load.at[1]),
        pltpu.make_async_copy(sizes_hbm, sizes_ref, load.at[2]),
    ]
    def block_at(x, at, far):
        one = (x + 4 - at % 4) % 4
        off = (4 * one + 2 + 32 - at) % 32
        return (one + 4 * (((off + 7) % 32) // 16) + 4 * far) % 8

    callers = [(2 * (8 * layer + 4 * core + i // 2) + i % 2, pan, rep) for i in range(8)]
    callers += [(2 * (8 * rep + 4 * core + i // 2) + i % 2, pan, layer) for i in range(8)]
    callers += [(wide, pan, (rep + step) % 4) for step in range(1, 4)]
    callers += [(wide, (pan + step) % 4, rep) for step in range(1, 4)]
    callers += [(2 * z + 1 - core, pan, rep)]
    callers += [(2 * (4 * owner + (layer + step) % 4) + core, pan, rep) for step in range(1, 4)]
    callers += [(2 * (4 * owner + rep) + b // 4, b % 4, layer) for b in range(8)]
    callers += [(2 * (4 * block_at(pan, z, far) + band) + rank // 4, z % 4, rep) for far in range(2)]
    barrier = pltpu.get_barrier_semaphore()
    for to in callers:
        pl.semaphore_signal(barrier, inc=1, device_id=device(*to), device_id_type=MESH)
    for copy in loads:
        copy.start()

    row_at = wide * 24 + lax.broadcasted_iota(jnp.int32, (24, 128), 0)
    lane = lax.broadcasted_iota(jnp.int32, (24, 128), 1)
    sum_at = (pan * 4 + rep) * 96 + lane
    lane8 = lane[0:8]

    def pack(value):
        last = value[16:24]
        pairs = jnp.where(lane8 < 32, pltpu.roll(last, 64, 1), pltpu.roll(pltpu.roll(last, 96, 1), 6, 0))
        pairs = jnp.where(lane8 < 64, pairs, pltpu.roll(last, 4, 0))
        pairs = jnp.where(lane8 < 96, pairs, pltpu.roll(pltpu.roll(last, 32, 1), 2, 0))
        return (
            jnp.where(lane8 < 96, value[0:8], pltpu.roll(last, 96, 1)),
            jnp.where(lane8 < 96, value[8:16], pltpu.roll(last, 64, 1)),
            pairs[0:2],
        )

    def unpack(one, two, tail):
        tail = jnp.concatenate([tail, jnp.zeros((6, 128), jnp.float32)], axis=0)
        last = pltpu.roll(tail, 64, 1) + pltpu.roll(pltpu.roll(tail, 32, 1), 2, 0)
        last = last + pltpu.roll(tail, 4, 0) + pltpu.roll(pltpu.roll(tail, 96, 1), 6, 0)
        last = jnp.where(lane8 < 64, pltpu.roll(two, 64, 1), last)
        return one, two, jnp.where(lane8 < 32, pltpu.roll(one, 32, 1), last)

    for copy in loads:
        copy.wait()
    for h in range(8):
        live = (row_at < sizes_ref[h]) & (sum_at < sizes_ref[h]) & (lane < 96)
        for side, ref in enumerate((amp_ref, int_ref)):
            value = jnp.concatenate([ref[h], jnp.zeros((24, 32), jnp.float32)], axis=1)
            value = jnp.where(live, value, 0.0)
            for row, part_of in zip((0, 8, 16), pack(value)):
                stage[side, h, row:row + part_of.shape[0]] = part_of
    pl.semaphore_wait(barrier, len(callers))

    slot1 = (rank % 4) * 2 + core
    for step in (4, 3, 5, 2, 6, 1, 7, 0):
        h = (owner + step) % 8
        to = (2 * (4 * h + rep) + rank // 4, pan, band)
        send_or_keep(stage.at[1, h], int_packed.at[rank // 4, rep, slot1], send1.at[1, step], recv1.at[1, slot1], to)
    for step in (4, 3, 5, 2, 6, 1, 7, 0):
        h = (owner + step) % 8
        to = (2 * (4 * h + band) + rank // 4, pan, rep)
        send_or_keep(stage.at[0, h], amp_packed.at[rep, slot1], send1.at[0, step], recv1.at[0, slot1], to)

    sibling = (2 * z + 1 - core, pan, rep)
    for pair in range(4):
        two = slice(2 * pair, 2 * pair + 2)
        for i in (2 * pair, 2 * pair + 1):
            arrived(int_packed.at[core, layer, i], recv1.at[1, i])
        here = int_packed.at[core, layer, two]
        for step in (2, 1, 3):
            to = (2 * (4 * owner + (layer + step) % 4) + core, pan, rep)
            send(here, here, send_b.at[pair, step], recv_b.at[pair, layer], to)
        send(here, here, send_c.at[pair, 0], recv_c.at[pair, layer], sibling)
    for pair in range(4):
        two = slice(2 * pair, 2 * pair + 2)
        for i in (2 * pair, 2 * pair + 1):
            arrived(amp_packed.at[rep, i], recv1.at[0, i])
        here = amp_packed.at[rep, two]
        for step in (2, 1, 3):
            send(here, here, send_a.at[pair, step], recv_a.at[pair, rep], (wide, pan, (rep + step) % 4))

    def spread(packed, whole, index, mask):
        for i in range(8):
            values = unpack(*(packed[index + (i, slice(*rows))] for rows in ((0, 8), (8, 16), (16, 18))))
            for row, value in zip((0, 8, 16), values):
                whole[index + (slice(24 * i + row, 24 * i + row + 8),)] = jnp.where(lane8 < 96, value, 0.0) if mask else value

    spread(int_packed, int_all, (core, layer), False)
    for step in (1, 3, 2):
        l = (layer + step) % 4
        for pair in range(4):
            two = slice(2 * pair, 2 * pair + 2)
            here = int_packed.at[core, l, two]
            arrived(here, recv_b.at[pair, l])
            send(here, here, send_c.at[pair, step], recv_c.at[pair, l], sibling)
        spread(int_packed, int_all, (core, l), False)
    spread(amp_packed, amp_all, (rep,), True)
    for step in (0, 1, 3, 2):
        l = (layer + step) % 4
        for pair in range(4):
            arrived(int_packed.at[1 - core, l, 2 * pair:2 * pair + 2], recv_c.at[pair, l])
        spread(int_packed, int_all, (1 - core, l), False)
    for step in (1, 3, 2):
        y = (rep + step) % 4
        for pair in range(4):
            arrived(amp_packed.at[y, 2 * pair:2 * pair + 2], recv_a.at[pair, y])
        spread(amp_packed, amp_all, (y,), True)

    for side in range(2):
        total = jnp.zeros((192, 192), jnp.float32)
        for y in range(4):
            total = total + lax.dot_general(
                amp_all[y], int_all[side, y],
                (((1,), (1,)), ((), ())), precision=lax.Precision.HIGHEST, preferred_element_type=jnp.float32,
            )
        part[:, 192 * side:192 * (side + 1)] = total
    for step in (2, 1, 3):
        x = (pan + step) % 4
        rows = part.at[pl.ds(pl.multiple_of(48 * x, 8), 48)]
        send(rows, parts.at[pan], send3.at[step], recv3.at[pan], (wide, x, rep))
    parts[pan] = part[pl.ds(pl.multiple_of(48 * pan, 8), 48)]
    for step in range(1, 4):
        x = (pan + step) % 4
        arrived(parts.at[x], recv3.at[x])
    cycle = parts[0] + parts[1] + parts[2] + parts[3]

    flipped = jnp.concatenate([cycle, jnp.zeros((80, 384), jnp.float32)], axis=0).T.reshape(8, 2, 24, 128)
    right = pltpu.roll(flipped[:, 1].reshape(192, 128), 48, 1)
    paired = flipped[:, 0] + right.reshape(8, 24, 128)
    for b in range(8):
        for row, part_of in zip((0, 8, 16), pack(paired[b])):
            block_out[b, row:row + part_of.shape[0]] = part_of
    mine = 4 * core + pan
    for step in range(8):
        b = (mine + step) % 8
        to = (2 * (4 * owner + rep) + b // 4, b % 4, layer)
        send_or_keep(block_out.at[b], block_in.at[mine], send4.at[step], recv4.at[mine], to)
    top, bottom = jnp.zeros((24, 384), jnp.float32), jnp.zeros((24, 384), jnp.float32)
    wide_lane = lax.broadcasted_iota(jnp.int32, (24, 384), 1)
    for b in range(8):
        arrived(block_in.at[b], recv4.at[b])
        both = jnp.concatenate(unpack(block_in[b, 0:8], block_in[b, 8:16], block_in[b, 16:18]), axis=0)
        both = jnp.concatenate([jnp.where(lane < 96, both, 0.0), jnp.zeros((24, 256), jnp.float32)], axis=1)
        above = jnp.where(wide_lane < 48, both, 0.0)
        top = top + (pltpu.roll(above, 48 * b, 1) if b else above)
        below = both - above
        bottom = bottom + (pltpu.roll(below, (48 * b + 336) % 384, 1) if b != 1 else below)
    rows_out[0:24] = -(cycle[0:24] + top)
    rows_out[24:48] = -(cycle[24:48] + bottom)

    columns = pl.ds(pl.multiple_of(384 * rep, 128), 384)
    goal = 8 * layer + 4 * core + pan
    column = (owner + pan) % 4
    far = ((owner + 8 - block_at(column, goal, 0)) % 8) // 4
    for c in range(2):
        to = (2 * goal + c, column, rep)
        send_or_keep(rows_out.at[24 * c:24 * (c + 1)], out_ref.at[owner, :, columns], send5.at[c], recv5.at[far], to)

    def place(i, j):
        return (pan + i * core + j * (1 - core)) % 4, (rep + i * (1 - core) + j * core) % 4

    def rows(half, i, j):
        x, y = place(i, j)
        return out_ref.at[block_at(x, z, half), :, pl.ds(pl.multiple_of(384 * y, 128), 384)]

    def to_neighbours(half, i):
        here = rows(half, i, 0)
        if i == 2:
            send(here, here, send8.at[half, 2], recv8.at[half, 2], (wide,) + place(0, 2))
        for way in (1, 3):
            send(here, here, send7.at[half, way // 2, i], recv7.at[half, way // 2, i], (wide,) + place(0, way))

    for half in range(2):
        here = rows(half, 0, 0)
        arrived(here, recv5.at[half])
        for i in (2, 1, 3):
            send(here, here, send6.at[half, i], recv6.at[half, 4 - i], (wide,) + place(i, 0))
        to_neighbours(half, 0)
        for i in (1, 3, 2):
            arrived(rows(half, i, 0), recv6.at[half, i])
            to_neighbours(half, i)
        for i in (0, 1, 3):
            come, go = (1, 3) if i < 2 else (3, 1)
            here = rows(half, i, come)
            arrived(here, recv7.at[half, 1 if i < 2 else 0, i])
            send(here, here, send8.at[half, i], recv8.at[half, i], (wide,) + place(0, go))
    for half in range(2):
        for i in range(4):
            if i != 2:
                arrived(rows(half, i, 3 if i < 2 else 1), recv7.at[half, 0 if i < 2 else 1, i])
            else:
                arrived(rows(half, i, 3), recv7.at[half, 0, i])
                arrived(rows(half, i, 1), recv7.at[half, 1, i])
            arrived(rows(half, i, 2), recv8.at[half, i])

    for args in sent:
        remote(*args).wait_send()
    for args in sent_or_kept:
        finish_send(*args)


def shards(amplitudes, integrals, pair_energies, block_sizes):
    vmem = pl.BlockSpec(memory_space=pltpu.VMEM)
    hbm = pl.BlockSpec(memory_space=pltpu.HBM)
    dma = pltpu.SemaphoreType.DMA
    negated = pl.pallas_call(
        cycle_kernel,
        out_shape=jax.ShapeDtypeStruct((8, 24, 1536), jnp.float32),
        in_specs=[hbm, hbm, hbm],
        out_specs=vmem,
        scratch_shapes=[
            pltpu.SMEM((8,), jnp.int32),
            pltpu.VMEM((8, 24, 96), jnp.float32),
            pltpu.VMEM((8, 24, 96), jnp.float32),
            pltpu.VMEM((2, 8, 18, 128), jnp.float32),
            pltpu.VMEM((4, 8, 18, 128), jnp.float32),
            pltpu.VMEM((2, 4, 8, 18, 128), jnp.float32),
            pltpu.VMEM((4, 192, 128), jnp.float32),
            pltpu.VMEM((2, 4, 192, 128), jnp.float32),
            pltpu.VMEM((192, 384), jnp.float32),
            pltpu.VMEM((4, 48, 384), jnp.float32),
            pltpu.VMEM((8, 18, 128), jnp.float32),
            pltpu.VMEM((8, 18, 128), jnp.float32),
            pltpu.VMEM((48, 384), jnp.float32),
            dma((3,)), dma((2, 8)), dma((2, 8)),
            dma((4, 4)), dma((4, 4)), dma((4, 4)), dma((4, 4)), dma((4, 4)), dma((4, 4)),
            dma((4,)), dma((4,)), dma((8,)), dma((8,)), dma((2,)), dma((2,)),
            dma((2, 4)), dma((2, 4)), dma((2, 2, 4)), dma((2, 2, 4)), dma((2, 4)), dma((2, 4)),
        ],
        compiler_params=pltpu.CompilerParams(collective_id=0, has_side_effects=True, vmem_limit_bytes=24 * 1024 * 1024),
        cost_estimate=pl.CostEstimate(flops=60_000_000, bytes_accessed=2_000_000, transcendentals=0),
    )(*(pltpu.with_memory_space_constraint(operand, pltpu.HBM) for operand in (block_sizes, amplitudes, jnp.swapaxes(integrals, 1, 2))))
    negated, pair_energies = lax.optimization_barrier((negated, pair_energies))
    row_start = lax.axis_index("wide") * 24
    energy_rows = lax.dynamic_slice_in_dim(pair_energies, row_start, 24, 1)
    update = negated / (energy_rows[:, :, None] + pair_energies[:, None, :])
    return (-negated, update)


def solution(mesh):
    in_specs = (P(None, "wide", ("pan", "rep")), P(None, ("pan", "rep"), "wide"), P(), P())
    out_specs = (P(None, "wide", None), P(None, "wide", None))
    return jax.shard_map(shards, mesh=mesh, in_specs=in_specs, out_specs=out_specs, check_vma=False)
```

```python
import jax
import jax.numpy as jnp
from jax import lax
from jax.experimental import pallas as pl
from jax.experimental.pallas import tpu as pltpu
from jax.sharding import PartitionSpec as P

MESH = pl.DeviceIdType.MESH


def cycle_kernel(
    sizes_hbm, amp_hbm, int_hbm, out_ref,
    sizes_ref, amp_ref, int_ref, stage, amp_packed, int_packed, amp_all, int_all, part, parts, block_out, block_in, rows_out,
    load, send1, recv1, send_a, recv_a, send_b, recv_b, send_c, recv_c,
    send3, recv3, send4, recv4, send5, recv5, send6, recv6, send7, recv7, send8, recv8,
):
    wide, pan, rep = lax.axis_index("wide"), lax.axis_index("pan"), lax.axis_index("rep")
    z, core = wide // 2, wide % 2
    owner, layer = z // 4, z % 4
    band, rank = z // 8, z % 8

    def device(w, x, y):
        return {"wide": w, "pan": x, "rep": y}

    def remote(src, dst, ssem, rsem, to):
        return pltpu.make_async_remote_copy(
            src_ref=src, dst_ref=dst, send_sem=ssem, recv_sem=rsem,
            device_id=device(*to), device_id_type=MESH,
        )

    def is_me(to):
        return (to[0] == wide) & (to[1] == pan) & (to[2] == rep)

    def start(src, dst, ssem, rsem, to):
        me = is_me(to)

        @pl.when(me)
        def _():
            pltpu.make_async_copy(src, dst, rsem).start()

        @pl.when(jnp.logical_not(me))
        def _():
            remote(src, dst, ssem, rsem, to).start()

    def finish_send(src, dst, ssem, rsem, to):
        @pl.when(jnp.logical_not(is_me(to)))
        def _():
            remote(src, dst, ssem, rsem, to).wait_send()

    def arrived(dst, rsem):
        pltpu.make_async_copy(dst, dst, rsem).wait()

    sent, sent_or_kept = [], []

    def send(*args):
        sent.append(args)
        remote(*args).start()

    def send_or_keep(*args):
        sent_or_kept.append(args)
        start(*args)

    loads = [
        pltpu.make_async_copy(amp_hbm, amp_ref, load.at[0]),
        pltpu.make_async_copy(int_hbm, int_ref, load.at[1]),
        pltpu.make_async_copy(sizes_hbm, sizes_ref, load.at[2]),
    ]
    def block_at(x, at, far):
        one = (x + 4 - at % 4) % 4
        off = (4 * one + 2 + 32 - at) % 32
        return (one + 4 * (((off + 7) % 32) // 16) + 4 * far) % 8

    callers = [(2 * (8 * layer + 4 * core + i // 2) + i % 2, pan, rep) for i in range(8)]
    callers += [(2 * (8 * rep + 4 * core + i // 2) + i % 2, pan, layer) for i in range(8)]
    callers += [(wide, pan, (rep + step) % 4) for step in range(1, 4)]
    callers += [(wide, (pan + step) % 4, rep) for step in range(1, 4)]
    callers += [(2 * z + 1 - core, pan, rep)]
    callers += [(2 * (4 * owner + (layer + step) % 4) + core, pan, rep) for step in range(1, 4)]
    callers += [(2 * (4 * owner + rep) + b // 4, b % 4, layer) for b in range(8)]
    callers += [(2 * (4 * block_at(pan, z, far) + band) + rank // 4, z % 4, rep) for far in range(2)]
    barrier = pltpu.get_barrier_semaphore()
    for to in callers:
        pl.semaphore_signal(barrier, inc=1, device_id=device(*to), device_id_type=MESH)
    for copy in loads:
        copy.start()

    row_at = wide * 24 + lax.broadcasted_iota(jnp.int32, (24, 128), 0)
    lane = lax.broadcasted_iota(jnp.int32, (24, 128), 1)
    sum_at = (pan * 4 + rep) * 96 + lane
    lane8 = lane[0:8]

    def pack(value):
        last = value[16:24]
        pairs = jnp.where(lane8 < 32, pltpu.roll(last, 64, 1), pltpu.roll(pltpu.roll(last, 96, 1), 6, 0))
        pairs = jnp.where(lane8 < 64, pairs, pltpu.roll(last, 4, 0))
        pairs = jnp.where(lane8 < 96, pairs, pltpu.roll(pltpu.roll(last, 32, 1), 2, 0))
        return (
            jnp.where(lane8 < 96, value[0:8], pltpu.roll(last, 96, 1)),
            jnp.where(lane8 < 96, value[8:16], pltpu.roll(last, 64, 1)),
            pairs[0:2],
        )

    def unpack(one, two, tail):
        tail = jnp.concatenate([tail, jnp.zeros((6, 128), jnp.float32)], axis=0)
        last = pltpu.roll(tail, 64, 1) + pltpu.roll(pltpu.roll(tail, 32, 1), 2, 0)
        last = last + pltpu.roll(tail, 4, 0) + pltpu.roll(pltpu.roll(tail, 96, 1), 6, 0)
        last = jnp.where(lane8 < 64, pltpu.roll(two, 64, 1), last)
        return one, two, jnp.where(lane8 < 32, pltpu.roll(one, 32, 1), last)

    for copy in loads:
        copy.wait()
    for h in range(8):
        live = (row_at < sizes_ref[h]) & (sum_at < sizes_ref[h]) & (lane < 96)
        for side, ref in enumerate((amp_ref, int_ref)):
            value = jnp.concatenate([ref[h], jnp.zeros((24, 32), jnp.float32)], axis=1)
            value = jnp.where(live, value, 0.0)
            for row, part_of in zip((0, 8, 16), pack(value)):
                stage[side, h, row:row + part_of.shape[0]] = part_of
    pl.semaphore_wait(barrier, len(callers))

    slot1 = (rank % 4) * 2 + core
    for step in (4, 3, 5, 2, 6, 1, 7, 0):
        h = (owner + step) % 8
        to = (2 * (4 * h + rep) + rank // 4, pan, band)
        send_or_keep(stage.at[1, h], int_packed.at[rank // 4, rep, slot1], send1.at[1, step], recv1.at[1, slot1], to)
    for step in (4, 3, 5, 2, 6, 1, 7, 0):
        h = (owner + step) % 8
        to = (2 * (4 * h + band) + rank // 4, pan, rep)
        send_or_keep(stage.at[0, h], amp_packed.at[rep, slot1], send1.at[0, step], recv1.at[0, slot1], to)

    sibling = (2 * z + 1 - core, pan, rep)
    for pair in range(4):
        two = slice(2 * pair, 2 * pair + 2)
        for i in (2 * pair, 2 * pair + 1):
            arrived(int_packed.at[core, layer, i], recv1.at[1, i])
        here = int_packed.at[core, layer, two]
        for step in (2, 1, 3):
            to = (2 * (4 * owner + (layer + step) % 4) + core, pan, rep)
            send(here, here, send_b.at[pair, step], recv_b.at[pair, layer], to)
        send(here, here, send_c.at[pair, 0], recv_c.at[pair, layer], sibling)
    for pair in range(4):
        two = slice(2 * pair, 2 * pair + 2)
        for i in (2 * pair, 2 * pair + 1):
            arrived(amp_packed.at[rep, i], recv1.at[0, i])
        here = amp_packed.at[rep, two]
        for step in (2, 1, 3):
            send(here, here, send_a.at[pair, step], recv_a.at[pair, rep], (wide, pan, (rep + step) % 4))

    def spread(packed, index, whole, to, start_row, mask):
        for i in range(8):
            values = unpack(*(packed[index + (i, slice(*rows))] for rows in ((0, 8), (8, 16), (16, 18))))
            for row, value in zip((0, 8, 16), values):
                at = pl.ds(pl.multiple_of(start_row + 24 * i + row, 8), 8)
                whole[to, at] = jnp.where(lane8 < 96, value, 0.0) if mask else value

    def product(rows, y):
        return lax.dot_general(
            amp_all[y, rows], int_all[y], (((1,), (1,)), ((), ())),
            precision=lax.Precision.HIGHEST, preferred_element_type=jnp.float32,
        )

    spread(int_packed, (core, layer), int_all, layer, 192 * core, False)
    for step in (1, 3, 2):
        l = (layer + step) % 4
        for pair in range(4):
            two = slice(2 * pair, 2 * pair + 2)
            here = int_packed.at[core, l, two]
            arrived(here, recv_b.at[pair, l])
            send(here, here, send_c.at[pair, step], recv_c.at[pair, l], sibling)
        spread(int_packed, (core, l), int_all, l, 192 * core, False)
    spread(amp_packed, (rep,), amp_all, rep, 0, True)
    for step in (0, 1, 3, 2):
        l = (layer + step) % 4
        for pair in range(4):
            arrived(int_packed.at[1 - core, l, 2 * pair:2 * pair + 2], recv_c.at[pair, l])
        spread(int_packed, (1 - core, l), int_all, l, 192 * (1 - core), False)

    part[...] = product(slice(None), rep)
    for step in (1, 3, 2):
        y = (rep + step) % 4
        for pair in range(4):
            arrived(amp_packed.at[y, 2 * pair:2 * pair + 2], recv_a.at[pair, y])
        spread(amp_packed, (y,), amp_all, y, 0, True)
        if step != 2:
            part[...] += product(slice(None), y)
    for step in (2, 1, 3, 0):
        x = (pan + step) % 4
        rows = pl.ds(pl.multiple_of(48 * x, 8), 48)
        part[rows] += product(rows, (rep + 2) % 4)
        if step:
            send(part.at[rows], parts.at[pan], send3.at[step], recv3.at[pan], (wide, x, rep))
    parts[pan] = part[pl.ds(pl.multiple_of(48 * pan, 8), 48)]
    for step in range(1, 4):
        x = (pan + step) % 4
        arrived(parts.at[x], recv3.at[x])
    cycle = parts[0] + parts[1] + parts[2] + parts[3]

    flipped = jnp.concatenate([cycle, jnp.zeros((80, 384), jnp.float32)], axis=0).T.reshape(8, 2, 24, 128)
    right = pltpu.roll(flipped[:, 1].reshape(192, 128), 48, 1)
    paired = flipped[:, 0] + right.reshape(8, 24, 128)
    for b in range(8):
        for row, part_of in zip((0, 8, 16), pack(paired[b])):
            block_out[b, row:row + part_of.shape[0]] = part_of
    mine = 4 * core + pan
    for step in range(8):
        b = (mine + step) % 8
        to = (2 * (4 * owner + rep) + b // 4, b % 4, layer)
        send_or_keep(block_out.at[b], block_in.at[mine], send4.at[step], recv4.at[mine], to)
    top, bottom = jnp.zeros((24, 384), jnp.float32), jnp.zeros((24, 384), jnp.float32)
    wide_lane = lax.broadcasted_iota(jnp.int32, (24, 384), 1)
    for b in range(8):
        arrived(block_in.at[b], recv4.at[b])
        both = jnp.concatenate(unpack(block_in[b, 0:8], block_in[b, 8:16], block_in[b, 16:18]), axis=0)
        both = jnp.concatenate([jnp.where(lane < 96, both, 0.0), jnp.zeros((24, 256), jnp.float32)], axis=1)
        above = jnp.where(wide_lane < 48, both, 0.0)
        top = top + (pltpu.roll(above, 48 * b, 1) if b else above)
        below = both - above
        bottom = bottom + (pltpu.roll(below, (48 * b + 336) % 384, 1) if b != 1 else below)
    rows_out[0:24] = -(cycle[0:24] + top)
    rows_out[24:48] = -(cycle[24:48] + bottom)

    columns = pl.ds(pl.multiple_of(384 * rep, 128), 384)
    goal = 8 * layer + 4 * core + pan
    column = (owner + pan) % 4
    far = ((owner + 8 - block_at(column, goal, 0)) % 8) // 4
    for c in range(2):
        to = (2 * goal + c, column, rep)
        send_or_keep(rows_out.at[24 * c:24 * (c + 1)], out_ref.at[owner, :, columns], send5.at[c], recv5.at[far], to)

    def place(i, j):
        return (pan + i * core + j * (1 - core)) % 4, (rep + i * (1 - core) + j * core) % 4

    def rows(half, i, j):
        x, y = place(i, j)
        return out_ref.at[block_at(x, z, half), :, pl.ds(pl.multiple_of(384 * y, 128), 384)]

    def to_neighbours(half, i):
        here = rows(half, i, 0)
        if i == 2:
            send(here, here, send8.at[half, 2], recv8.at[half, 2], (wide,) + place(0, 2))
        for way in (1, 3):
            send(here, here, send7.at[half, way // 2, i], recv7.at[half, way // 2, i], (wide,) + place(0, way))

    for half in range(2):
        here = rows(half, 0, 0)
        arrived(here, recv5.at[half])
        for i in (2, 1, 3):
            send(here, here, send6.at[half, i], recv6.at[half, 4 - i], (wide,) + place(i, 0))
        to_neighbours(half, 0)
        for i in (1, 3, 2):
            arrived(rows(half, i, 0), recv6.at[half, i])
            to_neighbours(half, i)
        for i in (0, 1, 3):
            come, go = (1, 3) if i < 2 else (3, 1)
            here = rows(half, i, come)
            arrived(here, recv7.at[half, 1 if i < 2 else 0, i])
            send(here, here, send8.at[half, i], recv8.at[half, i], (wide,) + place(0, go))
    for half in range(2):
        for i in range(4):
            if i != 2:
                arrived(rows(half, i, 3 if i < 2 else 1), recv7.at[half, 0 if i < 2 else 1, i])
            else:
                arrived(rows(half, i, 3), recv7.at[half, 0, i])
                arrived(rows(half, i, 1), recv7.at[half, 1, i])
            arrived(rows(half, i, 2), recv8.at[half, i])

    for args in sent:
        remote(*args).wait_send()
    for args in sent_or_kept:
        finish_send(*args)


def shards(amplitudes, integrals, pair_energies, block_sizes):
    vmem = pl.BlockSpec(memory_space=pltpu.VMEM)
    hbm = pl.BlockSpec(memory_space=pltpu.HBM)
    dma = pltpu.SemaphoreType.DMA
    negated = pl.pallas_call(
        cycle_kernel,
        out_shape=jax.ShapeDtypeStruct((8, 24, 1536), jnp.float32),
        in_specs=[hbm, hbm, hbm],
        out_specs=vmem,
        scratch_shapes=[
            pltpu.SMEM((8,), jnp.int32),
            pltpu.VMEM((8, 24, 96), jnp.float32),
            pltpu.VMEM((8, 24, 96), jnp.float32),
            pltpu.VMEM((2, 8, 18, 128), jnp.float32),
            pltpu.VMEM((4, 8, 18, 128), jnp.float32),
            pltpu.VMEM((2, 4, 8, 18, 128), jnp.float32),
            pltpu.VMEM((4, 192, 128), jnp.float32),
            pltpu.VMEM((4, 384, 128), jnp.float32),
            pltpu.VMEM((192, 384), jnp.float32),
            pltpu.VMEM((4, 48, 384), jnp.float32),
            pltpu.VMEM((8, 18, 128), jnp.float32),
            pltpu.VMEM((8, 18, 128), jnp.float32),
            pltpu.VMEM((48, 384), jnp.float32),
            dma((3,)), dma((2, 8)), dma((2, 8)),
            dma((4, 4)), dma((4, 4)), dma((4, 4)), dma((4, 4)), dma((4, 4)), dma((4, 4)),
            dma((4,)), dma((4,)), dma((8,)), dma((8,)), dma((2,)), dma((2,)),
            dma((2, 4)), dma((2, 4)), dma((2, 2, 4)), dma((2, 2, 4)), dma((2, 4)), dma((2, 4)),
        ],
        compiler_params=pltpu.CompilerParams(collective_id=0, has_side_effects=True, vmem_limit_bytes=24 * 1024 * 1024),
        cost_estimate=pl.CostEstimate(flops=60_000_000, bytes_accessed=2_000_000, transcendentals=0),
    )(*(pltpu.with_memory_space_constraint(operand, pltpu.HBM) for operand in (block_sizes, amplitudes, jnp.swapaxes(integrals, 1, 2))))
    negated, pair_energies = lax.optimization_barrier((negated, pair_energies))
    row_start = lax.axis_index("wide") * 24
    energy_rows = lax.dynamic_slice_in_dim(pair_energies, row_start, 24, 1)
    update = negated / (energy_rows[:, :, None] + pair_energies[:, None, :])
    return (-negated, update)


def solution(mesh):
    in_specs = (P(None, "wide", ("pan", "rep")), P(None, ("pan", "rep"), "wide"), P(), P())
    out_specs = (P(None, "wide", None), P(None, "wide", None))
    return jax.shard_map(shards, mesh=mesh, in_specs=in_specs, out_specs=out_specs, check_vma=False)
```

```python
import jax
import jax.numpy as jnp
from jax import lax
from jax.experimental import pallas as pl
from jax.experimental.pallas import tpu as pltpu
from jax.sharding import PartitionSpec as P

MESH = pl.DeviceIdType.MESH


def cycle_kernel(
    sizes_hbm, amp_hbm, int_hbm, out_ref,
    sizes_ref, amp_ref, int_ref, stage, amp_packed, int_packed, amp_all, int_all, part, parts, block_out, block_in, rows_out,
    load, send1, recv1, send_a, recv_a, send_b, recv_b, send_c, recv_c,
    send3, recv3, send4, recv4, send5, recv5, send6, recv6, send7, recv7, send8, recv8,
):
    wide, pan, rep = lax.axis_index("wide"), lax.axis_index("pan"), lax.axis_index("rep")
    z, core = wide // 2, wide % 2
    owner, layer = z // 4, z % 4
    band, rank = z // 8, z % 8

    def device(w, x, y):
        return {"wide": w, "pan": x, "rep": y}

    def remote(src, dst, ssem, rsem, to):
        return pltpu.make_async_remote_copy(
            src_ref=src, dst_ref=dst, send_sem=ssem, recv_sem=rsem,
            device_id=device(*to), device_id_type=MESH,
        )

    def is_me(to):
        return (to[0] == wide) & (to[1] == pan) & (to[2] == rep)

    def start(src, dst, ssem, rsem, to):
        me = is_me(to)

        @pl.when(me)
        def _():
            pltpu.make_async_copy(src, dst, rsem).start()

        @pl.when(jnp.logical_not(me))
        def _():
            remote(src, dst, ssem, rsem, to).start()

    def finish_send(src, dst, ssem, rsem, to):
        @pl.when(jnp.logical_not(is_me(to)))
        def _():
            remote(src, dst, ssem, rsem, to).wait_send()

    def drain(list_of_sends, finish):
        for args in list_of_sends:
            finish(*args)
        list_of_sends.clear()

    def arrived(dst, rsem):
        pltpu.make_async_copy(dst, dst, rsem).wait()

    sent, sent_or_kept = [], []

    def send(*args):
        sent.append(args)
        remote(*args).start()

    def send_or_keep(*args):
        sent_or_kept.append(args)
        start(*args)

    loads = [
        pltpu.make_async_copy(amp_hbm, amp_ref, load.at[0]),
        pltpu.make_async_copy(int_hbm, int_ref, load.at[1]),
        pltpu.make_async_copy(sizes_hbm, sizes_ref, load.at[2]),
    ]
    def block_at(x, at, far):
        one = (x + 4 - at % 4) % 4
        off = (4 * one + 2 + 32 - at) % 32
        return (one + 4 * (((off + 7) % 32) // 16) + 4 * far) % 8

    callers = [(2 * (8 * layer + 4 * core + i // 2) + i % 2, pan, rep) for i in range(8)]
    callers += [(2 * (8 * rep + 4 * core + i // 2) + i % 2, pan, layer) for i in range(8)]
    callers += [(wide, pan, (rep + step) % 4) for step in range(1, 4)]
    callers += [(wide, (pan + step) % 4, rep) for step in range(1, 4)]
    callers += [(2 * z + 1 - core, pan, rep)]
    callers += [(2 * (4 * owner + (layer + step) % 4) + core, pan, rep) for step in range(1, 4)]
    callers += [(2 * (4 * owner + rep) + b // 4, b % 4, layer) for b in range(8)]
    callers += [(2 * (4 * block_at(pan, z, far) + band) + rank // 4, z % 4, rep) for far in range(2)]
    barrier = pltpu.get_barrier_semaphore()
    for to in callers:
        pl.semaphore_signal(barrier, inc=1, device_id=device(*to), device_id_type=MESH)
    for copy in loads:
        copy.start()

    row_at = wide * 24 + lax.broadcasted_iota(jnp.int32, (24, 128), 0)
    lane = lax.broadcasted_iota(jnp.int32, (24, 128), 1)
    sum_at = (pan * 4 + rep) * 96 + lane
    lane8 = lane[0:8]

    def pack(value):
        last = value[16:24]
        pairs = jnp.where(lane8 < 32, pltpu.roll(last, 64, 1), pltpu.roll(pltpu.roll(last, 96, 1), 6, 0))
        pairs = jnp.where(lane8 < 64, pairs, pltpu.roll(last, 4, 0))
        pairs = jnp.where(lane8 < 96, pairs, pltpu.roll(pltpu.roll(last, 32, 1), 2, 0))
        return (
            jnp.where(lane8 < 96, value[0:8], pltpu.roll(last, 96, 1)),
            jnp.where(lane8 < 96, value[8:16], pltpu.roll(last, 64, 1)),
            pairs[0:2],
        )

    def unpack(one, two, tail):
        tail = jnp.concatenate([tail, jnp.zeros((6, 128), jnp.float32)], axis=0)
        last = pltpu.roll(tail, 64, 1) + pltpu.roll(pltpu.roll(tail, 32, 1), 2, 0)
        last = last + pltpu.roll(tail, 4, 0) + pltpu.roll(pltpu.roll(tail, 96, 1), 6, 0)
        last = jnp.where(lane8 < 64, pltpu.roll(two, 64, 1), last)
        return one, two, jnp.where(lane8 < 32, pltpu.roll(one, 32, 1), last)

    for copy in loads:
        copy.wait()
    for h in range(8):
        live = (row_at < sizes_ref[h]) & (sum_at < sizes_ref[h]) & (lane < 96)
        for side, ref in enumerate((amp_ref, int_ref)):
            value = jnp.concatenate([ref[h], jnp.zeros((24, 32), jnp.float32)], axis=1)
            value = jnp.where(live, value, 0.0)
            for row, part_of in zip((0, 8, 16), pack(value)):
                stage[side, h, row:row + part_of.shape[0]] = part_of
    pl.semaphore_wait(barrier, len(callers))

    slot1 = (rank % 4) * 2 + core
    for step in (4, 3, 5, 2, 6, 1, 7, 0):
        h = (owner + step) % 8
        to = (2 * (4 * h + rep) + rank // 4, pan, band)
        send_or_keep(stage.at[1, h], int_packed.at[rank // 4, rep, slot1], send1.at[1, step], recv1.at[1, slot1], to)
    for step in (4, 3, 5, 2, 6, 1, 7, 0):
        h = (owner + step) % 8
        to = (2 * (4 * h + band) + rank // 4, pan, rep)
        send_or_keep(stage.at[0, h], amp_packed.at[rep, slot1], send1.at[0, step], recv1.at[0, slot1], to)

    sibling = (2 * z + 1 - core, pan, rep)
    for pair in range(4):
        two = slice(2 * pair, 2 * pair + 2)
        for i in (2 * pair, 2 * pair + 1):
            arrived(int_packed.at[core, layer, i], recv1.at[1, i])
        here = int_packed.at[core, layer, two]
        for step in (2, 1, 3):
            to = (2 * (4 * owner + (layer + step) % 4) + core, pan, rep)
            send(here, here, send_b.at[pair, step], recv_b.at[pair, layer], to)
        send(here, here, send_c.at[pair, 0], recv_c.at[pair, layer], sibling)
    for pair in range(4):
        two = slice(2 * pair, 2 * pair + 2)
        for i in (2 * pair, 2 * pair + 1):
            arrived(amp_packed.at[rep, i], recv1.at[0, i])
        here = amp_packed.at[rep, two]
        for step in (2, 1, 3):
            send(here, here, send_a.at[pair, step], recv_a.at[pair, rep], (wide, pan, (rep + step) % 4))

    def spread(packed, index, whole, to, start_row, mask):
        for i in range(8):
            values = unpack(*(packed[index + (i, slice(*rows))] for rows in ((0, 8), (8, 16), (16, 18))))
            for row, value in zip((0, 8, 16), values):
                at = pl.ds(pl.multiple_of(start_row + 24 * i + row, 8), 8)
                whole[to, at] = jnp.where(lane8 < 96, value, 0.0) if mask else value

    def product(rows, y):
        return lax.dot_general(
            amp_all[y, rows], int_all[y], (((1,), (1,)), ((), ())),
            precision=lax.Precision.HIGHEST, preferred_element_type=jnp.float32,
        )

    spread(int_packed, (core, layer), int_all, layer, 192 * core, False)
    for step in (1, 3, 2):
        l = (layer + step) % 4
        for pair in range(4):
            two = slice(2 * pair, 2 * pair + 2)
            here = int_packed.at[core, l, two]
            arrived(here, recv_b.at[pair, l])
            send(here, here, send_c.at[pair, step], recv_c.at[pair, l], sibling)
        spread(int_packed, (core, l), int_all, l, 192 * core, False)
    spread(amp_packed, (rep,), amp_all, rep, 0, True)
    for step in (0, 1, 3, 2):
        l = (layer + step) % 4
        for pair in range(4):
            arrived(int_packed.at[1 - core, l, 2 * pair:2 * pair + 2], recv_c.at[pair, l])
        spread(int_packed, (1 - core, l), int_all, l, 192 * (1 - core), False)

    part[...] = product(slice(None), rep)
    for step in (1, 3, 2):
        y = (rep + step) % 4
        for pair in range(4):
            arrived(amp_packed.at[y, 2 * pair:2 * pair + 2], recv_a.at[pair, y])
        spread(amp_packed, (y,), amp_all, y, 0, True)
        if step != 2:
            part[...] += product(slice(None), y)
    for step in (2, 1, 3, 0):
        x = (pan + step) % 4
        rows = pl.ds(pl.multiple_of(48 * x, 8), 48)
        part[rows] += product(rows, (rep + 2) % 4)
        if step:
            send(part.at[rows], parts.at[pan], send3.at[step], recv3.at[pan], (wide, x, rep))
    parts[pan] = part[pl.ds(pl.multiple_of(48 * pan, 8), 48)]
    for step in range(1, 4):
        x = (pan + step) % 4
        arrived(parts.at[x], recv3.at[x])
    cycle = parts[0] + parts[1] + parts[2] + parts[3]

    flipped = jnp.concatenate([cycle, jnp.zeros((80, 384), jnp.float32)], axis=0).T.reshape(8, 2, 24, 128)
    right = pltpu.roll(flipped[:, 1].reshape(192, 128), 48, 1)
    paired = flipped[:, 0] + right.reshape(8, 24, 128)
    for b in range(8):
        for row, part_of in zip((0, 8, 16), pack(paired[b])):
            block_out[b, row:row + part_of.shape[0]] = part_of
    mine = 4 * core + pan
    for step in range(8):
        b = (mine + step) % 8
        to = (2 * (4 * owner + rep) + b // 4, b % 4, layer)
        send_or_keep(block_out.at[b], block_in.at[mine], send4.at[step], recv4.at[mine], to)
    top, bottom = jnp.zeros((24, 384), jnp.float32), jnp.zeros((24, 384), jnp.float32)
    wide_lane = lax.broadcasted_iota(jnp.int32, (24, 384), 1)
    for b in range(8):
        arrived(block_in.at[b], recv4.at[b])
        both = jnp.concatenate(unpack(block_in[b, 0:8], block_in[b, 8:16], block_in[b, 16:18]), axis=0)
        both = jnp.concatenate([jnp.where(lane < 96, both, 0.0), jnp.zeros((24, 256), jnp.float32)], axis=1)
        above = jnp.where(wide_lane < 48, both, 0.0)
        top = top + (pltpu.roll(above, 48 * b, 1) if b else above)
        below = both - above
        bottom = bottom + (pltpu.roll(below, (48 * b + 336) % 384, 1) if b != 1 else below)
    rows_out[0:24] = -(cycle[0:24] + top)
    rows_out[24:48] = -(cycle[24:48] + bottom)

    columns = pl.ds(pl.multiple_of(384 * rep, 128), 384)
    earlier, earlier_or_kept = sent[:], sent_or_kept[:]
    sent.clear()
    sent_or_kept.clear()
    goal = 8 * layer + 4 * core + pan
    column = (owner + pan) % 4
    far = ((owner + 8 - block_at(column, goal, 0)) % 8) // 4
    for c in range(2):
        to = (2 * goal + c, column, rep)
        send_or_keep(rows_out.at[24 * c:24 * (c + 1)], out_ref.at[owner, :, columns], send5.at[c], recv5.at[far], to)

    drain(earlier, lambda *args: remote(*args).wait_send())
    drain(earlier_or_kept, finish_send)

    def place(i, j):
        return (pan + i * core + j * (1 - core)) % 4, (rep + i * (1 - core) + j * core) % 4

    def rows(half, i, j):
        x, y = place(i, j)
        return out_ref.at[block_at(x, z, half), :, pl.ds(pl.multiple_of(384 * y, 128), 384)]

    def to_neighbours(half, i):
        here = rows(half, i, 0)
        if i == 2:
            send(here, here, send8.at[half, 2], recv8.at[half, 2], (wide,) + place(0, 2))
        for way in (1, 3):
            send(here, here, send7.at[half, way // 2, i], recv7.at[half, way // 2, i], (wide,) + place(0, way))

    for half in range(2):
        here = rows(half, 0, 0)
        arrived(here, recv5.at[half])
        for i in (2, 1, 3):
            send(here, here, send6.at[half, i], recv6.at[half, 4 - i], (wide,) + place(i, 0))
        to_neighbours(half, 0)
        for i in (1, 3, 2):
            arrived(rows(half, i, 0), recv6.at[half, i])
            to_neighbours(half, i)
        for i in (0, 1, 3):
            come, go = (1, 3) if i < 2 else (3, 1)
            here = rows(half, i, come)
            arrived(here, recv7.at[half, 1 if i < 2 else 0, i])
            send(here, here, send8.at[half, i], recv8.at[half, i], (wide,) + place(0, go))
        if half == 0:
            near_sends = sent[:]
            sent.clear()
    drain(near_sends, lambda *args: remote(*args).wait_send())
    drain(sent_or_kept, finish_send)
    for half in range(2):
        for i in range(4):
            if i != 2:
                arrived(rows(half, i, 3 if i < 2 else 1), recv7.at[half, 0 if i < 2 else 1, i])
            else:
                arrived(rows(half, i, 3), recv7.at[half, 0, i])
                arrived(rows(half, i, 1), recv7.at[half, 1, i])
            arrived(rows(half, i, 2), recv8.at[half, i])

    drain(sent, lambda *args: remote(*args).wait_send())


def shards(amplitudes, integrals, pair_energies, block_sizes):
    vmem = pl.BlockSpec(memory_space=pltpu.VMEM)
    hbm = pl.BlockSpec(memory_space=pltpu.HBM)
    dma = pltpu.SemaphoreType.DMA
    negated = pl.pallas_call(
        cycle_kernel,
        out_shape=jax.ShapeDtypeStruct((8, 24, 1536), jnp.float32),
        in_specs=[hbm, hbm, hbm],
        out_specs=vmem,
        scratch_shapes=[
            pltpu.SMEM((8,), jnp.int32),
            pltpu.VMEM((8, 24, 96), jnp.float32),
            pltpu.VMEM((8, 24, 96), jnp.float32),
            pltpu.VMEM((2, 8, 18, 128), jnp.float32),
            pltpu.VMEM((4, 8, 18, 128), jnp.float32),
            pltpu.VMEM((2, 4, 8, 18, 128), jnp.float32),
            pltpu.VMEM((4, 192, 128), jnp.float32),
            pltpu.VMEM((4, 384, 128), jnp.float32),
            pltpu.VMEM((192, 384), jnp.float32),
            pltpu.VMEM((4, 48, 384), jnp.float32),
            pltpu.VMEM((8, 18, 128), jnp.float32),
            pltpu.VMEM((8, 18, 128), jnp.float32),
            pltpu.VMEM((48, 384), jnp.float32),
            dma((3,)), dma((2, 8)), dma((2, 8)),
            dma((4, 4)), dma((4, 4)), dma((4, 4)), dma((4, 4)), dma((4, 4)), dma((4, 4)),
            dma((4,)), dma((4,)), dma((8,)), dma((8,)), dma((2,)), dma((2,)),
            dma((2, 4)), dma((2, 4)), dma((2, 2, 4)), dma((2, 2, 4)), dma((2, 4)), dma((2, 4)),
        ],
        compiler_params=pltpu.CompilerParams(collective_id=0, has_side_effects=True, vmem_limit_bytes=24 * 1024 * 1024),
        cost_estimate=pl.CostEstimate(flops=60_000_000, bytes_accessed=2_000_000, transcendentals=0),
    )(*(pltpu.with_memory_space_constraint(operand, pltpu.HBM) for operand in (block_sizes, amplitudes, jnp.swapaxes(integrals, 1, 2))))
    negated, pair_energies = lax.optimization_barrier((negated, pair_energies))
    row_start = lax.axis_index("wide") * 24
    energy_rows = lax.dynamic_slice_in_dim(pair_energies, row_start, 24, 1)
    update = negated / (energy_rows[:, :, None] + pair_energies[:, None, :])
    return (-negated, update)


def solution(mesh):
    in_specs = (P(None, "wide", ("pan", "rep")), P(None, ("pan", "rep"), "wide"), P(), P())
    out_specs = (P(None, "wide", None), P(None, "wide", None))
    return jax.shard_map(shards, mesh=mesh, in_specs=in_specs, out_specs=out_specs, check_vma=False)
```

```python
import jax
import jax.numpy as jnp
from jax import lax
from jax.experimental import pallas as pl
from jax.experimental.pallas import tpu as pltpu
from jax.sharding import PartitionSpec as P

MESH = pl.DeviceIdType.MESH


def cycle_kernel(
    sizes_hbm, amp_hbm, int_hbm, out_ref,
    sizes_ref, amp_ref, int_ref, stage, amp_packed, int_packed, amp_all, int_all, part, parts, block_out, block_in, rows_out,
    load, send1, recv1, send_a, recv_a, send_b, recv_b, send_c, recv_c,
    send3, recv3, send4, recv4, send5, recv5, send6, recv6, send7, recv7, send8, recv8,
):
    wide, pan, rep = lax.axis_index("wide"), lax.axis_index("pan"), lax.axis_index("rep")
    z, core = wide // 2, wide % 2
    owner, layer = z // 4, z % 4
    band, rank = z // 8, z % 8

    def device(w, x, y):
        return {"wide": w, "pan": x, "rep": y}

    def remote(src, dst, ssem, rsem, to):
        return pltpu.make_async_remote_copy(
            src_ref=src, dst_ref=dst, send_sem=ssem, recv_sem=rsem,
            device_id=device(*to), device_id_type=MESH,
        )

    def is_me(to):
        return (to[0] == wide) & (to[1] == pan) & (to[2] == rep)

    def start(src, dst, ssem, rsem, to):
        me = is_me(to)

        @pl.when(me)
        def _():
            pltpu.make_async_copy(src, dst, rsem).start()

        @pl.when(jnp.logical_not(me))
        def _():
            remote(src, dst, ssem, rsem, to).start()

    def finish_send(src, dst, ssem, rsem, to):
        @pl.when(jnp.logical_not(is_me(to)))
        def _():
            remote(src, dst, ssem, rsem, to).wait_send()

    def drain(list_of_sends, finish):
        for args in list_of_sends:
            finish(*args)
        list_of_sends.clear()

    def arrived(dst, rsem):
        pltpu.make_async_copy(dst, dst, rsem).wait()

    sent, sent_or_kept = [], []

    def send(*args):
        sent.append(args)
        remote(*args).start()

    def send_or_keep(*args):
        sent_or_kept.append(args)
        start(*args)

    loads = [
        pltpu.make_async_copy(amp_hbm, amp_ref, load.at[0]),
        pltpu.make_async_copy(int_hbm, int_ref, load.at[1]),
        pltpu.make_async_copy(sizes_hbm, sizes_ref, load.at[2]),
    ]
    def block_at(x, at, far):
        one = (x + 4 - at % 4) % 4
        off = (4 * one + 2 + 32 - at) % 32
        return (one + 4 * (((off + 7) % 32) // 16) + 4 * far) % 8

    callers = [(2 * (8 * layer + 4 * core + i // 2) + i % 2, pan, rep) for i in range(8)]
    callers += [(2 * (8 * rep + 4 * core + i // 2) + i % 2, pan, layer) for i in range(8)]
    callers += [(wide, pan, (rep + step) % 4) for step in range(1, 4)]
    callers += [(wide, (pan + step) % 4, rep) for step in range(1, 4)]
    callers += [(2 * z + 1 - core, pan, rep)]
    callers += [(2 * (4 * owner + (layer + step) % 4) + core, pan, rep) for step in range(1, 4)]
    callers += [(2 * (4 * owner + rep) + b // 4, b % 4, layer) for b in range(8)]
    callers += [(2 * (4 * block_at(pan, z, far) + band) + rank // 4, z % 4, rep) for far in range(2)]
    barrier = pltpu.get_barrier_semaphore()
    for to in callers:
        pl.semaphore_signal(barrier, inc=1, device_id=device(*to), device_id_type=MESH)
    for copy in loads:
        copy.start()

    row_at = wide * 24 + lax.broadcasted_iota(jnp.int32, (24, 128), 0)
    lane = lax.broadcasted_iota(jnp.int32, (24, 128), 1)
    sum_at = (pan * 4 + rep) * 96 + lane
    lane8 = lane[0:8]

    def pack(value):
        last = value[16:24]
        pairs = jnp.where(lane8 < 32, pltpu.roll(last, 64, 1), pltpu.roll(pltpu.roll(last, 96, 1), 6, 0))
        pairs = jnp.where(lane8 < 64, pairs, pltpu.roll(last, 4, 0))
        pairs = jnp.where(lane8 < 96, pairs, pltpu.roll(pltpu.roll(last, 32, 1), 2, 0))
        return (
            jnp.where(lane8 < 96, value[0:8], pltpu.roll(last, 96, 1)),
            jnp.where(lane8 < 96, value[8:16], pltpu.roll(last, 64, 1)),
            pairs[0:2],
        )

    def unpack(one, two, tail):
        tail = jnp.concatenate([tail, jnp.zeros((6, 128), jnp.float32)], axis=0)
        last = pltpu.roll(tail, 64, 1) + pltpu.roll(pltpu.roll(tail, 32, 1), 2, 0)
        last = last + pltpu.roll(tail, 4, 0) + pltpu.roll(pltpu.roll(tail, 96, 1), 6, 0)
        last = jnp.where(lane8 < 64, pltpu.roll(two, 64, 1), last)
        return one, two, jnp.where(lane8 < 32, pltpu.roll(one, 32, 1), last)

    for copy in loads:
        copy.wait()
    for h in range(8):
        live = (row_at < sizes_ref[h]) & (sum_at < sizes_ref[h]) & (lane < 96)
        for side, ref in enumerate((amp_ref, int_ref)):
            value = jnp.concatenate([ref[h], jnp.zeros((24, 32), jnp.float32)], axis=1)
            value = jnp.where(live, value, 0.0)
            for row, part_of in zip((0, 8, 16), pack(value)):
                stage[side, h, row:row + part_of.shape[0]] = part_of
    pl.semaphore_wait(barrier, len(callers))

    slot1 = (rank % 4) * 2 + core
    for step in (4, 3, 5, 2, 6, 1, 7, 0):
        h = (owner + step) % 8
        to = (2 * (4 * h + rep) + rank // 4, pan, band)
        send_or_keep(stage.at[1, h], int_packed.at[rank // 4, rep, slot1], send1.at[1, step], recv1.at[1, slot1], to)
    for step in (4, 3, 5, 2, 6, 1, 7, 0):
        h = (owner + step) % 8
        to = (2 * (4 * h + band) + rank // 4, pan, rep)
        send_or_keep(stage.at[0, h], amp_packed.at[rep, slot1], send1.at[0, step], recv1.at[0, slot1], to)

    sibling = (2 * z + 1 - core, pan, rep)
    for pair in range(4):
        two = slice(2 * pair, 2 * pair + 2)
        for i in (2 * pair, 2 * pair + 1):
            arrived(int_packed.at[core, layer, i], recv1.at[1, i])
        here = int_packed.at[core, layer, two]
        for step in (2, 1, 3):
            to = (2 * (4 * owner + (layer + step) % 4) + core, pan, rep)
            send(here, here, send_b.at[pair, step], recv_b.at[pair, layer], to)
        send(here, here, send_c.at[pair, 0], recv_c.at[pair, layer], sibling)
    for pair in range(4):
        two = slice(2 * pair, 2 * pair + 2)
        for i in (2 * pair, 2 * pair + 1):
            arrived(amp_packed.at[rep, i], recv1.at[0, i])
        here = amp_packed.at[rep, two]
        for step in (2, 1, 3):
            send(here, here, send_a.at[pair, step], recv_a.at[pair, rep], (wide, pan, (rep + step) % 4))

    def spread(packed, index, whole, to, start_row, mask):
        for i in range(8):
            values = unpack(*(packed[index + (i, slice(*rows))] for rows in ((0, 8), (8, 16), (16, 18))))
            for row, value in zip((0, 8, 16), values):
                at = pl.ds(pl.multiple_of(start_row + 24 * i + row, 8), 8)
                whole[to, at] = jnp.where(lane8 < 96, value, 0.0) if mask else value

    def product(rows, y):
        return lax.dot_general(
            amp_all[y, rows], int_all[y], (((1,), (1,)), ((), ())),
            precision=lax.Precision.HIGHEST, preferred_element_type=jnp.float32,
        )

    spread(int_packed, (core, layer), int_all, layer, 192 * core, False)
    for step in (1, 3, 2):
        l = (layer + step) % 4
        for pair in range(4):
            two = slice(2 * pair, 2 * pair + 2)
            here = int_packed.at[core, l, two]
            arrived(here, recv_b.at[pair, l])
            send(here, here, send_c.at[pair, step], recv_c.at[pair, l], sibling)
        spread(int_packed, (core, l), int_all, l, 192 * core, False)
    spread(amp_packed, (rep,), amp_all, rep, 0, True)
    for step in (0, 1, 3, 2):
        l = (layer + step) % 4
        for pair in range(4):
            arrived(int_packed.at[1 - core, l, 2 * pair:2 * pair + 2], recv_c.at[pair, l])
        spread(int_packed, (1 - core, l), int_all, l, 192 * (1 - core), False)

    part[...] = product(slice(None), rep)
    for step in (1, 3, 2):
        y = (rep + step) % 4
        for pair in range(4):
            arrived(amp_packed.at[y, 2 * pair:2 * pair + 2], recv_a.at[pair, y])
        spread(amp_packed, (y,), amp_all, y, 0, True)
        if step != 2:
            part[...] += product(slice(None), y)
    for step in (2, 1, 3, 0):
        x = (pan + step) % 4
        rows = pl.ds(pl.multiple_of(48 * x, 8), 48)
        part[rows] += product(rows, (rep + 2) % 4)
        if step:
            send(part.at[rows], parts.at[pan], send3.at[step], recv3.at[pan], (wide, x, rep))
    parts[pan] = part[pl.ds(pl.multiple_of(48 * pan, 8), 48)]
    for step in range(1, 4):
        x = (pan + step) % 4
        arrived(parts.at[x], recv3.at[x])
    cycle = parts[0] + parts[1] + parts[2] + parts[3]

    flipped = jnp.concatenate([cycle, jnp.zeros((80, 384), jnp.float32)], axis=0).T.reshape(8, 2, 24, 128)
    right = pltpu.roll(flipped[:, 1].reshape(192, 128), 48, 1)
    paired = flipped[:, 0] + right.reshape(8, 24, 128)
    for b in range(8):
        for row, part_of in zip((0, 8, 16), pack(paired[b])):
            block_out[b, row:row + part_of.shape[0]] = part_of
    mine = 4 * core + pan
    for step in range(8):
        b = (mine + step) % 8
        to = (2 * (4 * owner + rep) + b // 4, b % 4, layer)
        send_or_keep(block_out.at[b], block_in.at[mine], send4.at[step], recv4.at[mine], to)
    top, bottom = jnp.zeros((24, 384), jnp.float32), jnp.zeros((24, 384), jnp.float32)
    wide_lane = lax.broadcasted_iota(jnp.int32, (24, 384), 1)
    for b in range(8):
        arrived(block_in.at[b], recv4.at[b])
        both = jnp.concatenate(unpack(block_in[b, 0:8], block_in[b, 8:16], block_in[b, 16:18]), axis=0)
        both = jnp.concatenate([jnp.where(lane < 96, both, 0.0), jnp.zeros((24, 256), jnp.float32)], axis=1)
        above = jnp.where(wide_lane < 48, both, 0.0)
        top = top + (pltpu.roll(above, 48 * b, 1) if b else above)
        below = both - above
        bottom = bottom + (pltpu.roll(below, (48 * b + 336) % 384, 1) if b != 1 else below)
    rows_out[0:24] = -(cycle[0:24] + top)
    rows_out[24:48] = -(cycle[24:48] + bottom)

    columns = pl.ds(pl.multiple_of(384 * rep, 128), 384)
    earlier, earlier_or_kept = sent[:], sent_or_kept[:]
    sent.clear()
    sent_or_kept.clear()
    goal = 8 * layer + 4 * core + pan
    column = (owner + pan) % 4
    far = ((owner + 8 - block_at(column, goal, 0)) % 8) // 4
    for c in range(2):
        to = (2 * goal + c, column, rep)
        send_or_keep(rows_out.at[24 * c:24 * (c + 1)], out_ref.at[owner, :, columns], send5.at[c], recv5.at[far], to)

    drain(earlier, lambda *args: remote(*args).wait_send())
    drain(earlier_or_kept, finish_send)

    def place(i, j):
        return (pan + i * core + j * (1 - core)) % 4, (rep + i * (1 - core) + j * core) % 4

    def rows(half, i, j):
        x, y = place(i, j)
        return out_ref.at[block_at(x, z, half), :, pl.ds(pl.multiple_of(384 * y, 128), 384)]

    def straight(half, i):
        return i == 2 or (half == 1 and i > 0)

    def to_neighbours(half, i):
        here = rows(half, i, 0)
        if straight(half, i):
            send(here, here, send8.at[half, i], recv8.at[half, i], (wide,) + place(0, 2))
        for way in (1, 3):
            send(here, here, send7.at[half, way // 2, i], recv7.at[half, way // 2, i], (wide,) + place(0, way))

    for half in range(2):
        here = rows(half, 0, 0)
        arrived(here, recv5.at[half])
        for i in (2, 1, 3):
            send(here, here, send6.at[half, i], recv6.at[half, 4 - i], (wide,) + place(i, 0))
        to_neighbours(half, 0)
        for i in (1, 3, 2):
            arrived(rows(half, i, 0), recv6.at[half, i])
            to_neighbours(half, i)
        for i in (0,) if half else (0, 1, 3):
            come, go = (1, 3) if i < 2 else (3, 1)
            here = rows(half, i, come)
            arrived(here, recv7.at[half, 1 if i < 2 else 0, i])
            send(here, here, send8.at[half, i], recv8.at[half, i], (wide,) + place(0, go))
        if half == 0:
            near_sends = sent[:]
            sent.clear()
    drain(near_sends, lambda *args: remote(*args).wait_send())
    drain(sent_or_kept, finish_send)
    for half in range(2):
        for i in range(4):
            if not straight(half, i):
                arrived(rows(half, i, 3 if i < 2 else 1), recv7.at[half, 0 if i < 2 else 1, i])
            else:
                arrived(rows(half, i, 3), recv7.at[half, 0, i])
                arrived(rows(half, i, 1), recv7.at[half, 1, i])
            arrived(rows(half, i, 2), recv8.at[half, i])

    drain(sent, lambda *args: remote(*args).wait_send())


def shards(amplitudes, integrals, pair_energies, block_sizes):
    vmem = pl.BlockSpec(memory_space=pltpu.VMEM)
    hbm = pl.BlockSpec(memory_space=pltpu.HBM)
    dma = pltpu.SemaphoreType.DMA
    negated = pl.pallas_call(
        cycle_kernel,
        out_shape=jax.ShapeDtypeStruct((8, 24, 1536), jnp.float32),
        in_specs=[hbm, hbm, hbm],
        out_specs=vmem,
        scratch_shapes=[
            pltpu.SMEM((8,), jnp.int32),
            pltpu.VMEM((8, 24, 96), jnp.float32),
            pltpu.VMEM((8, 24, 96), jnp.float32),
            pltpu.VMEM((2, 8, 18, 128), jnp.float32),
            pltpu.VMEM((4, 8, 18, 128), jnp.float32),
            pltpu.VMEM((2, 4, 8, 18, 128), jnp.float32),
            pltpu.VMEM((4, 192, 128), jnp.float32),
            pltpu.VMEM((4, 384, 128), jnp.float32),
            pltpu.VMEM((192, 384), jnp.float32),
            pltpu.VMEM((4, 48, 384), jnp.float32),
            pltpu.VMEM((8, 18, 128), jnp.float32),
            pltpu.VMEM((8, 18, 128), jnp.float32),
            pltpu.VMEM((48, 384), jnp.float32),
            dma((3,)), dma((2, 8)), dma((2, 8)),
            dma((4, 4)), dma((4, 4)), dma((4, 4)), dma((4, 4)), dma((4, 4)), dma((4, 4)),
            dma((4,)), dma((4,)), dma((8,)), dma((8,)), dma((2,)), dma((2,)),
            dma((2, 4)), dma((2, 4)), dma((2, 2, 4)), dma((2, 2, 4)), dma((2, 4)), dma((2, 4)),
        ],
        compiler_params=pltpu.CompilerParams(collective_id=0, has_side_effects=True, vmem_limit_bytes=24 * 1024 * 1024),
        cost_estimate=pl.CostEstimate(flops=60_000_000, bytes_accessed=2_000_000, transcendentals=0),
    )(*(pltpu.with_memory_space_constraint(operand, pltpu.HBM) for operand in (block_sizes, amplitudes, jnp.swapaxes(integrals, 1, 2))))
    negated, pair_energies = lax.optimization_barrier((negated, pair_energies))
    row_start = lax.axis_index("wide") * 24
    energy_rows = lax.dynamic_slice_in_dim(pair_energies, row_start, 24, 1)
    update = negated / (energy_rows[:, :, None] + pair_energies[:, None, :])
    return (-negated, update)


def solution(mesh):
    in_specs = (P(None, "wide", ("pan", "rep")), P(None, ("pan", "rep"), "wide"), P(), P())
    out_specs = (P(None, "wide", None), P(None, "wide", None))
    return jax.shard_map(shards, mesh=mesh, in_specs=in_specs, out_specs=out_specs, check_vma=False)
```

```python
import jax
import jax.numpy as jnp
from jax import lax
from jax.experimental import pallas as pl
from jax.experimental.pallas import tpu as pltpu
from jax.sharding import PartitionSpec as P

MESH = pl.DeviceIdType.MESH


def cycle_kernel(
    sizes_hbm, amp_hbm, int_hbm, out_ref,
    sizes_ref, amp_ref, int_ref, stage, amp_packed, int_packed, amp_all, int_all, part, parts, block_out, block_in, rows_out,
    load, send1, recv1, send_a, recv_a, send_b, recv_b, send_c, recv_c,
    send3, recv3, send4, recv4, send5, recv5, send6, recv6, send7, recv7, send8, recv8,
):
    wide, pan, rep = lax.axis_index("wide"), lax.axis_index("pan"), lax.axis_index("rep")
    z, core = wide // 2, wide % 2
    owner, layer = z // 4, z % 4
    band, rank = z // 8, z % 8

    def device(w, x, y):
        return {"wide": w, "pan": x, "rep": y}

    def remote(src, dst, ssem, rsem, to):
        return pltpu.make_async_remote_copy(
            src_ref=src, dst_ref=dst, send_sem=ssem, recv_sem=rsem,
            device_id=device(*to), device_id_type=MESH,
        )

    def is_me(to):
        return (to[0] == wide) & (to[1] == pan) & (to[2] == rep)

    def start(src, dst, ssem, rsem, to):
        me = is_me(to)

        @pl.when(me)
        def _():
            pltpu.make_async_copy(src, dst, rsem).start()

        @pl.when(jnp.logical_not(me))
        def _():
            remote(src, dst, ssem, rsem, to).start()

    def finish_send(src, dst, ssem, rsem, to):
        @pl.when(jnp.logical_not(is_me(to)))
        def _():
            remote(src, dst, ssem, rsem, to).wait_send()

    def drain(list_of_sends, finish):
        for args in list_of_sends:
            finish(*args)
        list_of_sends.clear()

    def arrived(dst, rsem):
        pltpu.make_async_copy(dst, dst, rsem).wait()

    sent, sent_or_kept = [], []

    def send(*args):
        sent.append(args)
        remote(*args).start()

    def send_or_keep(*args):
        sent_or_kept.append(args)
        start(*args)

    loads = [
        pltpu.make_async_copy(amp_hbm, amp_ref, load.at[0]),
        pltpu.make_async_copy(int_hbm, int_ref, load.at[1]),
        pltpu.make_async_copy(sizes_hbm, sizes_ref, load.at[2]),
    ]
    def block_at(x, at, far):
        one = (x + 4 - at % 4) % 4
        off = (4 * one + 2 + 32 - at) % 32
        return (one + 4 * (((off + 7) % 32) // 16) + 4 * far) % 8

    callers = [(2 * (8 * layer + 4 * core + i // 2) + i % 2, pan, rep) for i in range(8)]
    callers += [(2 * (8 * rep + 4 * core + i // 2) + i % 2, pan, layer) for i in range(8)]
    callers += [(wide, pan, (rep + step) % 4) for step in range(1, 4)]
    callers += [(wide, (pan + step) % 4, rep) for step in range(1, 4)]
    callers += [(2 * z + 1 - core, pan, rep)]
    callers += [(2 * (4 * owner + (layer + step) % 4) + core, pan, rep) for step in range(1, 4)]
    callers += [(2 * (4 * owner + rep) + b // 4, b % 4, layer) for b in range(8)]
    callers += [(2 * (4 * block_at(pan, z, far) + band) + rank // 4, z % 4, rep) for far in range(2)]
    barrier = pltpu.get_barrier_semaphore()
    for to in callers:
        pl.semaphore_signal(barrier, inc=1, device_id=device(*to), device_id_type=MESH)
    for copy in loads:
        copy.start()

    row_at = wide * 24 + lax.broadcasted_iota(jnp.int32, (24, 128), 0)
    lane = lax.broadcasted_iota(jnp.int32, (24, 128), 1)
    sum_at = (pan * 4 + rep) * 96 + lane
    lane8 = lane[0:8]

    def pack(value):
        last = value[16:24]
        pairs = jnp.where(lane8 < 32, pltpu.roll(last, 64, 1), pltpu.roll(pltpu.roll(last, 96, 1), 6, 0))
        pairs = jnp.where(lane8 < 64, pairs, pltpu.roll(last, 4, 0))
        pairs = jnp.where(lane8 < 96, pairs, pltpu.roll(pltpu.roll(last, 32, 1), 2, 0))
        return (
            jnp.where(lane8 < 96, value[0:8], pltpu.roll(last, 96, 1)),
            jnp.where(lane8 < 96, value[8:16], pltpu.roll(last, 64, 1)),
            pairs[0:2],
        )

    def unpack(one, two, tail):
        tail = jnp.concatenate([tail, jnp.zeros((6, 128), jnp.float32)], axis=0)
        last = pltpu.roll(tail, 64, 1) + pltpu.roll(pltpu.roll(tail, 32, 1), 2, 0)
        last = last + pltpu.roll(tail, 4, 0) + pltpu.roll(pltpu.roll(tail, 96, 1), 6, 0)
        last = jnp.where(lane8 < 64, pltpu.roll(two, 64, 1), last)
        return one, two, jnp.where(lane8 < 32, pltpu.roll(one, 32, 1), last)

    for copy in loads:
        copy.wait()
    for h in range(8):
        live = (row_at < sizes_ref[h]) & (sum_at < sizes_ref[h]) & (lane < 96)
        for side, ref in enumerate((amp_ref, int_ref)):
            value = jnp.concatenate([ref[h], jnp.zeros((24, 32), jnp.float32)], axis=1)
            value = jnp.where(live, value, 0.0)
            for row, part_of in zip((0, 8, 16), pack(value)):
                stage[side, h, row:row + part_of.shape[0]] = part_of
    pl.semaphore_wait(barrier, len(callers))

    slot1 = (rank % 4) * 2 + core
    for step in (4, 3, 5, 2, 6, 1, 7, 0):
        h = (owner + step) % 8
        to = (2 * (4 * h + rep) + rank // 4, pan, band)
        send_or_keep(stage.at[1, h], int_packed.at[rank // 4, rep, slot1], send1.at[1, step], recv1.at[1, slot1], to)
    for step in (4, 3, 5, 2, 6, 1, 7, 0):
        h = (owner + step) % 8
        to = (2 * (4 * h + band) + rank // 4, pan, rep)
        send_or_keep(stage.at[0, h], amp_packed.at[rep, slot1], send1.at[0, step], recv1.at[0, slot1], to)

    sibling = (2 * z + 1 - core, pan, rep)
    for pair in range(4):
        two = slice(2 * pair, 2 * pair + 2)
        for i in (2 * pair, 2 * pair + 1):
            arrived(int_packed.at[core, layer, i], recv1.at[1, i])
        here = int_packed.at[core, layer, two]
        for step in (2, 1, 3):
            to = (2 * (4 * owner + (layer + step) % 4) + core, pan, rep)
            send(here, here, send_b.at[pair, step], recv_b.at[pair, layer], to)
        send(here, here, send_c.at[pair, 0], recv_c.at[pair, layer], sibling)
    for pair in range(4):
        two = slice(2 * pair, 2 * pair + 2)
        for i in (2 * pair, 2 * pair + 1):
            arrived(amp_packed.at[rep, i], recv1.at[0, i])
        here = amp_packed.at[rep, two]
        for step in (2, 1, 3):
            send(here, here, send_a.at[pair, step], recv_a.at[pair, rep], (wide, pan, (rep + step) % 4))

    def spread(packed, index, whole, to, start_row, mask):
        for i in range(8):
            values = unpack(*(packed[index + (i, slice(*rows))] for rows in ((0, 8), (8, 16), (16, 18))))
            for row, value in zip((0, 8, 16), values):
                at = pl.ds(pl.multiple_of(start_row + 24 * i + row, 8), 8)
                whole[to, at] = jnp.where(lane8 < 96, value, 0.0) if mask else value

    def product(rows, y):
        return lax.dot_general(
            amp_all[y, rows], int_all[y], (((1,), (1,)), ((), ())),
            precision=lax.Precision.HIGHEST, preferred_element_type=jnp.float32,
        )

    spread(int_packed, (core, layer), int_all, layer, 192 * core, False)
    for step in (1, 3, 2):
        l = (layer + step) % 4
        for pair in range(4):
            two = slice(2 * pair, 2 * pair + 2)
            here = int_packed.at[core, l, two]
            arrived(here, recv_b.at[pair, l])
            send(here, here, send_c.at[pair, step], recv_c.at[pair, l], sibling)
        spread(int_packed, (core, l), int_all, l, 192 * core, False)
    spread(amp_packed, (rep,), amp_all, rep, 0, True)
    for step in (0, 1, 3, 2):
        l = (layer + step) % 4
        for pair in range(4):
            arrived(int_packed.at[1 - core, l, 2 * pair:2 * pair + 2], recv_c.at[pair, l])
        spread(int_packed, (1 - core, l), int_all, l, 192 * (1 - core), False)

    part[...] = product(slice(None), rep)
    for step in (1, 3, 2):
        y = (rep + step) % 4
        for pair in range(4):
            arrived(amp_packed.at[y, 2 * pair:2 * pair + 2], recv_a.at[pair, y])
        spread(amp_packed, (y,), amp_all, y, 0, True)
        if step != 2:
            part[...] += product(slice(None), y)
    for step in (2, 1, 3, 0):
        x = (pan + step) % 4
        rows = pl.ds(pl.multiple_of(48 * x, 8), 48)
        part[rows] += product(rows, (rep + 2) % 4)
        if step:
            send(part.at[rows], parts.at[pan], send3.at[step], recv3.at[pan], (wide, x, rep))
    parts[pan] = part[pl.ds(pl.multiple_of(48 * pan, 8), 48)]
    for step in range(1, 4):
        x = (pan + step) % 4
        arrived(parts.at[x], recv3.at[x])
    cycle = parts[0] + parts[1] + parts[2] + parts[3]

    flipped = jnp.concatenate([cycle, jnp.zeros((80, 384), jnp.float32)], axis=0).T.reshape(8, 2, 24, 128)
    right = pltpu.roll(flipped[:, 1].reshape(192, 128), 48, 1)
    paired = flipped[:, 0] + right.reshape(8, 24, 128)
    for b in range(8):
        for row, part_of in zip((0, 8, 16), pack(paired[b])):
            block_out[b, row:row + part_of.shape[0]] = part_of
    mine = 4 * core + pan
    for step in range(8):
        b = (mine + step) % 8
        to = (2 * (4 * owner + rep) + b // 4, b % 4, layer)
        send_or_keep(block_out.at[b], block_in.at[mine], send4.at[step], recv4.at[mine], to)
    top, bottom = jnp.zeros((24, 384), jnp.float32), jnp.zeros((24, 384), jnp.float32)
    wide_lane = lax.broadcasted_iota(jnp.int32, (24, 384), 1)
    for b in range(8):
        arrived(block_in.at[b], recv4.at[b])
        both = jnp.concatenate(unpack(block_in[b, 0:8], block_in[b, 8:16], block_in[b, 16:18]), axis=0)
        both = jnp.concatenate([jnp.where(lane < 96, both, 0.0), jnp.zeros((24, 256), jnp.float32)], axis=1)
        above = jnp.where(wide_lane < 48, both, 0.0)
        top = top + (pltpu.roll(above, 48 * b, 1) if b else above)
        below = both - above
        bottom = bottom + (pltpu.roll(below, (48 * b + 336) % 384, 1) if b != 1 else below)
    rows_out[0:24] = -(cycle[0:24] + top)
    rows_out[24:48] = -(cycle[24:48] + bottom)

    columns = pl.ds(pl.multiple_of(384 * rep, 128), 384)
    earlier, earlier_or_kept = sent[:], sent_or_kept[:]
    sent.clear()
    sent_or_kept.clear()
    goal = 8 * layer + 4 * core + pan
    column = (owner + pan) % 4
    far = ((owner + 8 - block_at(column, goal, 0)) % 8) // 4
    for c in range(2):
        to = (2 * goal + c, column, rep)
        send_or_keep(rows_out.at[24 * c:24 * (c + 1)], out_ref.at[owner, :, columns], send5.at[c], recv5.at[far], to)

    drain(earlier, lambda *args: remote(*args).wait_send())
    drain(earlier_or_kept, finish_send)

    def place(i, j):
        return (pan + i * core + j * (1 - core)) % 4, (rep + i * (1 - core) + j * core) % 4

    def rows(half, i, j):
        x, y = place(i, j)
        return out_ref.at[block_at(x, z, half), :, pl.ds(pl.multiple_of(384 * y, 128), 384)]

    def straight(half, i):
        return i > 0

    def to_neighbours(half, i):
        here = rows(half, i, 0)
        if straight(half, i):
            send(here, here, send8.at[half, i], recv8.at[half, i], (wide,) + place(0, 2))
        for way in (1, 3):
            send(here, here, send7.at[half, way // 2, i], recv7.at[half, way // 2, i], (wide,) + place(0, way))

    for half in range(2):
        here = rows(half, 0, 0)
        arrived(here, recv5.at[half])
        for i in (2, 1, 3):
            send(here, here, send6.at[half, i], recv6.at[half, 4 - i], (wide,) + place(i, 0))
        to_neighbours(half, 0)
        for i in (1, 3, 2):
            arrived(rows(half, i, 0), recv6.at[half, i])
            to_neighbours(half, i)
        for i in (0,):
            come, go = (1, 3) if i < 2 else (3, 1)
            here = rows(half, i, come)
            arrived(here, recv7.at[half, 1 if i < 2 else 0, i])
            send(here, here, send8.at[half, i], recv8.at[half, i], (wide,) + place(0, go))
        if half == 0:
            near_sends = sent[:]
            sent.clear()
    drain(near_sends, lambda *args: remote(*args).wait_send())
    drain(sent_or_kept, finish_send)
    for half in range(2):
        for i in range(4):
            if not straight(half, i):
                arrived(rows(half, i, 3 if i < 2 else 1), recv7.at[half, 0 if i < 2 else 1, i])
            else:
                arrived(rows(half, i, 3), recv7.at[half, 0, i])
                arrived(rows(half, i, 1), recv7.at[half, 1, i])
            arrived(rows(half, i, 2), recv8.at[half, i])

    drain(sent, lambda *args: remote(*args).wait_send())


def shards(amplitudes, integrals, pair_energies, block_sizes):
    vmem = pl.BlockSpec(memory_space=pltpu.VMEM)
    hbm = pl.BlockSpec(memory_space=pltpu.HBM)
    dma = pltpu.SemaphoreType.DMA
    negated = pl.pallas_call(
        cycle_kernel,
        out_shape=jax.ShapeDtypeStruct((8, 24, 1536), jnp.float32),
        in_specs=[hbm, hbm, hbm],
        out_specs=vmem,
        scratch_shapes=[
            pltpu.SMEM((8,), jnp.int32),
            pltpu.VMEM((8, 24, 96), jnp.float32),
            pltpu.VMEM((8, 24, 96), jnp.float32),
            pltpu.VMEM((2, 8, 18, 128), jnp.float32),
            pltpu.VMEM((4, 8, 18, 128), jnp.float32),
            pltpu.VMEM((2, 4, 8, 18, 128), jnp.float32),
            pltpu.VMEM((4, 192, 128), jnp.float32),
            pltpu.VMEM((4, 384, 128), jnp.float32),
            pltpu.VMEM((192, 384), jnp.float32),
            pltpu.VMEM((4, 48, 384), jnp.float32),
            pltpu.VMEM((8, 18, 128), jnp.float32),
            pltpu.VMEM((8, 18, 128), jnp.float32),
            pltpu.VMEM((48, 384), jnp.float32),
            dma((3,)), dma((2, 8)), dma((2, 8)),
            dma((4, 4)), dma((4, 4)), dma((4, 4)), dma((4, 4)), dma((4, 4)), dma((4, 4)),
            dma((4,)), dma((4,)), dma((8,)), dma((8,)), dma((2,)), dma((2,)),
            dma((2, 4)), dma((2, 4)), dma((2, 2, 4)), dma((2, 2, 4)), dma((2, 4)), dma((2, 4)),
        ],
        compiler_params=pltpu.CompilerParams(collective_id=0, has_side_effects=True, vmem_limit_bytes=24 * 1024 * 1024),
        cost_estimate=pl.CostEstimate(flops=60_000_000, bytes_accessed=2_000_000, transcendentals=0),
    )(*(pltpu.with_memory_space_constraint(operand, pltpu.HBM) for operand in (block_sizes, amplitudes, jnp.swapaxes(integrals, 1, 2))))
    negated, pair_energies = lax.optimization_barrier((negated, pair_energies))
    row_start = lax.axis_index("wide") * 24
    energy_rows = lax.dynamic_slice_in_dim(pair_energies, row_start, 24, 1)
    update = negated / (energy_rows[:, :, None] + pair_energies[:, None, :])
    return (-negated, update)


def solution(mesh):
    in_specs = (P(None, "wide", ("pan", "rep")), P(None, ("pan", "rep"), "wide"), P(), P())
    out_specs = (P(None, "wide", None), P(None, "wide", None))
    return jax.shard_map(shards, mesh=mesh, in_specs=in_specs, out_specs=out_specs, check_vma=False)
```
